256 devices in a mesh: db: 32 (over y, z), tp: 8 (over x, core).
Axes of the slice: x: 4, y: 4, z: 8, core: 2. Of those that a mesh axis runs over, the one named last changes fastest.
Arguments:
- queries: bfloat16 [16384, 2048], P('db', 'tp'), may hold values from -400 to 400
- nbr_shard: int32 [256, 2], P('db'), may hold values from 0 to 31, all different within a row; in each aligned block of 8 rows (0 to 7, 8 to 15, ...) at most 2 rows name the same one
- nbr_row: int32 [256, 2], P('db'), may hold values from 0 to 3
- database: bfloat16 [128, 128, 4096], P('db', None, 'tp'), may hold values from -6 to 6
- key_weight: bfloat16 [4096, 2048], P(None, 'tp'), may hold values from -0.09375 to 0.09375
- value_weight: bfloat16 [4096, 2048], P(None, 'tp'), may hold values from -0.09375 to 0.09375
- lambda_head: float32 [8], P('tp'), may hold values from 0.1 to 0.9
- out_weight: bfloat16 [2048, 4096], P('tp'), may hold values from -0.125 to 0.125
Outputs:
- mixed_rows: bfloat16 [16384, 4096], P(('db', 'tp'))
The draws below stay inside these ranges and needn't reach their ends.
Inputs may be any that keep to these rules, and one draw needn't show every extreme that they name: `nbr_shard`: within the 8 rows of one device no shard is named more than 2 times, and in some device's rows one shard is named exactly 2 times; the 2 shards of a row differ.
All inputs are finite; a program needn't handle non-finite values.
Results may differ from the reference program's by a relative error of at most 0.019.
Values may be sent and summed in bfloat16 or wider, within the bound.
No kernel may reach another device: no remote copies, remote signals or barrier semaphores. Data moves between devices by JAX's collectives and lax.ppermute only.
A program may use at most 128 MiB of HBM per device.

```python
import math
import jax
import jax.numpy as jnp
import numpy as np
from jax import lax

D = 4096
HEADS = 8
HD = 128
SPAN = 64
NBR = 2
NLEN = 128
CH_DEV = 8
DB_DEV = 4
HEAD_GROUP = 1
CAP = 2
SPANS = 256
TOKENS = 16384
DB_ENTRIES = 128
N_DB = 32
N_TP = 8


def draw_queries(key, part):
    key = jax.random.fold_in(key, 7)
    normal_draw = jax.random.normal(key, (TOKENS, HEADS * 2 * HD), jnp.float32)
    return jnp.clip(normal_draw, -400.0, 400.0).astype(jnp.bfloat16)


def place_ends(array, stream_key, smallest, top_value):
    spot = [jax.random.randint(jax.random.fold_in(stream_key, axis), (), 0, length) for axis, length in enumerate(array.shape)]
    longest = array.shape.index(max(array.shape))
    beside = spot[:longest] + [(spot[longest] + 1) % array.shape[longest]] + spot[longest + 1:]
    return array.at[tuple(spot)].set(smallest).at[tuple(beside)].set(top_value)


def block_scale(stream_key, extent, shards, low, largest):
    def one(position, blocks):
        heights = jax.random.uniform(jax.random.fold_in(jax.random.fold_in(stream_key, 6), position), (blocks,), jnp.float32, low / len(shards), largest / len(shards))
        return jnp.repeat(jnp.exp(heights), extent[position] // blocks).reshape((-1,) + (1,) * (len(extent) - position - 1))

    level = one(*shards[0])
    for cut in shards[1:]:
        level = level * one(*cut)
    return level


def routed_block(own_key, own, number, rows, number_of, top, bound, lean):
    ranking = jax.random.permutation(own_key, number_of)
    packed, ordinary = shares(number_of, rows * top, bound, lean, True), shares(number_of, rows * top, bound, lean, False)
    places = jnp.arange(number_of)

    def named(lengths, rotation):
        used = int((lengths > 0).sum())
        fixed = max(1, used // 4)
        moved = fixed + (places - fixed + rotation * (used - fixed)) % max(1, number_of - fixed)
        return jnp.zeros((number_of,), jnp.int32).at[ranking[jnp.where(places < fixed, places, moved)]].set(jnp.asarray(lengths, jnp.int32))

    lengths = jnp.where(number % 4 == 0, named(packed, number // 4), named(ordinary, number - number // 4 - 1))
    mixed = jax.random.permutation(jax.random.fold_in(own, 3), number_of)
    donor, taker = mixed[0:number_of // 2 * 2:2], mixed[1:number_of // 2 * 2:2]
    slack = jnp.minimum(lengths[donor] - 1, bound - lengths[taker]) // 2
    slack = jnp.where((donor == ranking[0]) | (taker == ranking[0]) | (lengths[taker] == 0), 0, jnp.maximum(slack, 0))
    moved = jax.random.randint(jax.random.fold_in(own, 4), (number_of // 2,), 0, 1 << 20) % (slack + 1)
    lengths = lengths.at[donor].add(-moved).at[taker].add(moved)
    members = jnp.searchsorted(jnp.cumsum(lengths), jnp.arange(rows * top), side="right").astype(jnp.int32)
    listing = members.reshape(top, rows).T
    listing = listing[jax.random.permutation(jax.random.fold_in(own, 1), rows)]
    rotation = jax.random.randint(jax.random.fold_in(own, 2), (rows, 1), 0, top)
    return jnp.take_along_axis(listing, (jnp.arange(top)[None, :] + rotation) % top, axis=1)


def shares(amount, total, most, skew, full):
    weights = [(1 << 20) // math.isqrt(rank ** skew) + 1 for rank in range(1, amount + 1)]
    largest = most if full else min(most, max(-(-total // amount), total * weights[0] // sum(weights)))
    least = 1 if total - largest >= amount - 1 else 0
    given, surplus = [largest] + [least] * (amount - 1), total - largest - least * (amount - 1)
    while surplus > 0:
        candidates = [i for i in range(1, amount) if given[i] < largest] or [i for i in range(1, amount) if given[i] < most]
        pool, budget = sum([weights[i] for i in candidates]), surplus
        for i in candidates:
            more = min(most - given[i], max(1, budget * weights[i] // pool), surplus)
            given[i] = given[i] + more
            surplus = surplus - more
    return np.array(given)


def normal_values(key, shape, deviation, most, cuts=(), dtype=jnp.bfloat16):
    values = deviation * jax.random.normal(key, shape, jnp.float32)
    if cuts:
        values = values * block_scale(key, shape, cuts, -0.22, 0.18)
    return jnp.clip(values, -most, most).astype(dtype)


def setup_inputs(seed: int = 0) -> dict:
    splits = jax.random.split(jax.random.key(seed), 9)
    queries = draw_queries(jax.random.fold_in(splits[8], 71), 0)
    nbr_shard_keys = jax.random.split(jax.random.fold_in(splits[1], 1), SPANS // CH_DEV)
    nbr_shard_turns = jax.random.permutation(jax.random.fold_in(splits[1], 3), SPANS // CH_DEV)
    nbr_shard = jax.vmap(lambda own, number: routed_block(jax.random.fold_in(splits[1], 2), own, number, CH_DEV, N_DB, NBR, CAP, 2))(nbr_shard_keys, nbr_shard_turns).reshape((SPANS, NBR))
    nbr_row = place_ends(jax.random.randint(splits[2], (SPANS, NBR), 0, DB_DEV), jax.random.fold_in(splits[2], 1), 0, DB_DEV - 1).astype(jnp.int32)
    database = normal_values(splits[3], (DB_ENTRIES, NLEN, D), 1.0, 6.0, ((0, 32), (2, 8)))
    key_weight = normal_values(splits[4], (D, HEADS * 2 * HD), D ** -0.5, 0.09375, ((1, 8),))
    value_weight = normal_values(splits[5], (D, HEADS * 2 * HD), D ** -0.5, 0.09375, ((1, 8),))
    lambda_head = jnp.clip(0.1 + 0.79999997 * jax.random.uniform(splits[6], (HEADS,), jnp.float32) ** block_scale(splits[6], (HEADS,), ((0, 8),), -0.2, 0.2), 0.1, 0.9)
    out_weight = normal_values(splits[7], (HEADS * 2 * HD, D), (HEADS * 2 * HD) ** -0.5, 0.125, ((0, 8),))
    return {"queries": queries, "nbr_shard": nbr_shard, "nbr_row": nbr_row, "database": database, "key_weight": key_weight, "value_weight": value_weight, "lambda_head": lambda_head, "out_weight": out_weight}


EPSILON = 1e-05

def reference(queries, nbr_shard, nbr_row, database, key_weight, value_weight, lambda_head, out_weight):

    def encode_shard(entries):
        flat_rows = entries.reshape(DB_DEV * NLEN, D)
        as_float = flat_rows.astype(jnp.float32)
        inverse_rms = lax.rsqrt(lax.optimization_barrier(jnp.mean(as_float * as_float, axis=1, keepdims=True)) + EPSILON)
        key_rows = (jnp.dot(flat_rows, key_weight, preferred_element_type=jnp.float32) * inverse_rms).astype(jnp.bfloat16)
        value_rows = (jnp.dot(flat_rows, value_weight, preferred_element_type=jnp.float32) * inverse_rms).astype(jnp.bfloat16)
        return (key_rows.reshape(DB_DEV, NLEN, HEADS * 2 * HD), value_rows.reshape(DB_DEV, NLEN, HEADS * 2 * HD))
    key_table, value_table = lax.map(encode_shard, database.reshape(N_DB, DB_DEV, NLEN, D))
    key_table = key_table.reshape(DB_ENTRIES, NLEN, HEADS * 2 * HD)
    value_table = value_table.reshape(DB_ENTRIES, NLEN, HEADS * 2 * HD)
    entry = (nbr_shard * DB_DEV + nbr_row).astype(jnp.int32)

    def one_block(inputs):
        query_rows, block_ids = inputs
        key_blocks = key_table[block_ids].reshape(CH_DEV, NBR * NLEN, HEADS, 2, HD).astype(jnp.float32)
        value_blocks = value_table[block_ids].reshape(CH_DEV, NBR * NLEN, HEADS, 2 * HD).astype(jnp.float32)
        query_blocks = query_rows.reshape(CH_DEV, SPAN, HEADS, 2, HD).astype(jnp.float32)
        scores = jnp.einsum('cqhmd,clhmd->chmql', query_blocks, key_blocks) / HD ** 0.5
        probabilities = jax.nn.softmax(scores, axis=-1)
        mixing = (probabilities[:, :, 0] - lambda_head[None, :, None, None] * probabilities[:, :, 1]).astype(jnp.bfloat16)
        mixing = lax.optimization_barrier(mixing).astype(jnp.float32)
        attended = jnp.einsum('chql,clhe->cqhe', mixing, value_blocks)
        inverse_rms = lax.rsqrt(lax.optimization_barrier(jnp.mean(attended * attended, axis=-1, keepdims=True)) + EPSILON)
        heads_out = (attended * inverse_rms).astype(jnp.bfloat16).reshape(CH_DEV * SPAN, N_TP, HEAD_GROUP * 2 * HD)
        group_weight = out_weight.reshape(N_TP, HEAD_GROUP * 2 * HD, D).astype(jnp.float32)
        partial_value = jnp.einsum('rgc,gcd->grd', heads_out.astype(jnp.float32), group_weight)
        rounded = lax.optimization_barrier(partial_value.astype(jnp.bfloat16)).astype(jnp.float32)
        return lax.optimization_barrier(jnp.sum(rounded, axis=0)).astype(jnp.bfloat16)
    mixed_rows = lax.map(one_block, (queries.reshape(N_DB, CH_DEV * SPAN, HEADS * 2 * HD), entry.reshape(N_DB, CH_DEV, NBR)))
    return mixed_rows.reshape(TOKENS, D)
```

```python
import functools
import jax
import jax.numpy as jnp
from jax import lax
from jax.experimental import pallas as pl
from jax.experimental.pallas import tpu as pltpu
from jax.sharding import Mesh, PartitionSpec as P

HD = 128
SPAN = 64
NLEN = 128
EPSILON = 1e-05
FAR = -1e30
NY, NZ, NX, NC = 4, 8, 4, 2
SPANS_DEV = 8
ENTRIES = 4
CHUNKS = 2
EPC = ENTRIES // CHUNKS
ROWS = EPC * NLEN
QROWS = SPANS_DEV * SPAN
OROWS = 2 * QROWS
VMEM_LIMIT = 48 * 1024 * 1024


def shift(a, axis, k):
    n = lax.axis_size(axis)
    return lax.ppermute(a, axis, [(i, (i + k) % n) for i in range(n)])


def ring_pieces(a, axis):
    n = lax.axis_size(axis)
    half = a.shape[0] // 2
    out = [(0, 0, a)]
    up = down = a
    for k in range(1, (n - 1) // 2 + 1):
        up, down = shift(up, axis, 1), shift(down, axis, -1)
        out += [(k, 0, up), (n - k, 0, down)]
    out += [(n // 2, 0, shift(up[:half], axis, 1)), (n // 2, half, shift(down[half:], axis, -1))]
    return out


def project_kernel(layout, feature_ref, *refs):
    *pieces, key_ref, value_ref, out_ref = refs
    key_sum = value_sum = squares = None
    for block, members in enumerate(layout):
        rows = [pieces[i][...] for i in members]
        tokens = rows[0] if len(rows) == 1 else jnp.concatenate(rows, axis=0)
        width = tokens.shape[1]
        at = pl.ds(pl.multiple_of(feature_ref[block] * width, width), width)
        k = jnp.dot(tokens, key_ref[at, :], preferred_element_type=jnp.float32)
        v = jnp.dot(tokens, value_ref[at, :], preferred_element_type=jnp.float32)
        f = tokens.astype(jnp.float32)
        s = jnp.sum(f * f, axis=1, keepdims=True)
        if key_sum is None:
            key_sum, value_sum, squares = k, v, s
        else:
            key_sum, value_sum, squares = key_sum + k, value_sum + v, squares + s
    inverse = lax.rsqrt(squares / key_ref.shape[0] + EPSILON)
    out_ref[:, : 2 * HD] = (key_sum * inverse).astype(jnp.bfloat16)
    out_ref[:, 2 * HD :] = (value_sum * inverse).astype(jnp.bfloat16)


def project(feature, blocks, key_weight, value_weight):
    pieces, layout = [], []
    for members in blocks:
        layout.append(tuple(range(len(pieces), len(pieces) + len(members))))
        pieces += members
    vmem = pl.BlockSpec(memory_space=pltpu.VMEM)
    return pl.pallas_call(
        functools.partial(project_kernel, tuple(layout)),
        out_shape=jax.ShapeDtypeStruct((ROWS, 4 * HD), jnp.bfloat16),
        in_specs=[pl.BlockSpec(memory_space=pltpu.SMEM)] + [vmem] * (len(pieces) + 2),
        out_specs=vmem,
        compiler_params=pltpu.CompilerParams(vmem_limit_bytes=VMEM_LIMIT),
        cost_estimate=pl.CostEstimate(
            flops=2 * ROWS * 4096 * 512, bytes_accessed=6 << 20, transcendentals=0
        ),
        name="project",
    )(feature, *pieces, key_weight, value_weight)


def attend_kernel(places, offset_ref, active_ref, *refs):
    queries = refs[:NY]
    pieces = refs[NY : NY + len(places)]
    outs = refs[NY + len(places) : 2 * NY + len(places)]
    table, stats, sems = refs[2 * NY + len(places) :]
    copies = [
        pltpu.make_async_copy(piece, table.at[pl.ds(row, piece.shape[0])], sems.at[i])
        for i, (row, piece) in enumerate(zip(places, pieces))
    ]
    for copy in copies:
        copy.start()
    for copy in copies:
        copy.wait()
    key_row = lax.broadcasted_iota(jnp.int32, (2 * NLEN, 2 * SPAN), 0)
    lane = lax.broadcasted_iota(jnp.int32, (SPAN, 2 * HD), 1)
    for k in range(NY):

        def one_span(s, carry, k=k):
            at = (k * SPANS_DEV + s) * 2
            rows = [
                table[pl.ds(pl.multiple_of(offset_ref[at + j], NLEN), NLEN), :] for j in range(2)
            ]
            keys = jnp.concatenate([r[:, : 2 * HD] for r in rows], axis=0)
            values = jnp.concatenate([r[:, 2 * HD :] for r in rows], axis=0)
            q = queries[k][pl.ds(pl.multiple_of(s * SPAN, SPAN), SPAN), :]
            zero = jnp.zeros_like(q)
            both = jnp.concatenate(
                [jnp.where(lane < HD, q, zero), jnp.where(lane >= HD, q, zero)], axis=0
            )
            scores = (
                lax.dot_general(
                    keys, both, (((1,), (1,)), ((), ())), preferred_element_type=jnp.float32
                )
                / HD**0.5
            )
            here = jnp.where(key_row < NLEN, active_ref[at], active_ref[at + 1]) > 0
            scores = jnp.where(here, scores, FAR)
            top = jnp.max(scores, axis=0, keepdims=True)
            weight = jnp.exp(scores - top)
            total = jnp.sum(weight, axis=0, keepdims=True)
            stats[pl.ds(k * SPANS_DEV + s, 1), :] = top + jnp.log(total)
            share = (weight * (1.0 / total)).astype(jnp.bfloat16)
            outs[k][pl.ds(pl.multiple_of(s * 2 * SPAN, 2 * SPAN), 2 * SPAN), :] = lax.dot_general(
                share, values, (((0,), (0,)), ((), ())), preferred_element_type=jnp.float32
            ).astype(jnp.bfloat16)
            return carry

        lax.fori_loop(0, SPANS_DEV, one_span, 0, unroll=4)
        level = stats[k * SPANS_DEV : (k + 1) * SPANS_DEV, :]
        high = level.astype(jnp.bfloat16).astype(jnp.float32)
        rest = level - high
        mid = rest.astype(jnp.bfloat16).astype(jnp.float32)
        low = rest - mid
        coded = jnp.concatenate(
            [
                jnp.concatenate([high, mid], axis=1),
                jnp.concatenate([low, jnp.zeros_like(low)], axis=1),
            ],
            axis=0,
        )
        outs[k][OROWS : OROWS + 16, :] = coded.astype(jnp.bfloat16)


def attend(offsets, active, queries, pieces):
    places = tuple(row for row, _ in pieces)
    smem = pl.BlockSpec(memory_space=pltpu.SMEM)
    vmem = pl.BlockSpec(memory_space=pltpu.VMEM)
    return pl.pallas_call(
        functools.partial(attend_kernel, places),
        out_shape=[jax.ShapeDtypeStruct((OROWS + 16, 2 * HD), jnp.bfloat16)] * NY,
        in_specs=[smem, smem]
        + [vmem] * NY
        + [pl.BlockSpec(memory_space=pl.ANY)] * len(pieces),
        out_specs=[vmem] * NY,
        scratch_shapes=[
            pltpu.VMEM((NZ * ENTRIES * NLEN, 4 * HD), jnp.bfloat16),
            pltpu.VMEM((NY * SPANS_DEV, 2 * SPAN), jnp.float32),
            pltpu.SemaphoreType.DMA((len(pieces),)),
        ],
        compiler_params=pltpu.CompilerParams(vmem_limit_bytes=VMEM_LIMIT),
        cost_estimate=pl.CostEstimate(
            flops=2 << 30, bytes_accessed=8 << 20, transcendentals=1 << 20
        ),
        name="attend",
    )(offsets, active, *queries, *[a for _, a in pieces])


def combine_kernel(lambda_ref, *refs):
    *messages, out_ref = refs
    levels = []
    for message in messages:
        coded = message[OROWS : OROWS + 16, :].astype(jnp.float32)
        levels.append(
            (coded[:SPANS_DEV, : 2 * SPAN] + coded[:SPANS_DEV, 2 * SPAN :])
            + coded[SPANS_DEV:, : 2 * SPAN]
        )
    top = functools.reduce(jnp.maximum, levels)
    parts = [jnp.exp(level - top) for level in levels]
    total = functools.reduce(jnp.add, parts)
    lane = lax.broadcasted_iota(jnp.int32, (SPANS_DEV, 2 * SPAN), 1)
    sign = jnp.where(lane < SPAN, 1.0, -lambda_ref[0])
    factors = [part * (sign / total) for part in parts]
    column = lax.broadcasted_iota(jnp.int32, (SPAN, 2 * SPAN), 1) % SPAN
    row = lax.broadcasted_iota(jnp.int32, (SPAN, 2 * SPAN), 0)
    same = column == row
    for s in range(SPANS_DEV):
        attended = None
        for factor, message in zip(factors, messages):
            mix = jnp.where(same, factor[s : s + 1, :], 0.0).astype(jnp.bfloat16)
            term = jnp.dot(
                mix,
                message[s * 2 * SPAN : (s + 1) * 2 * SPAN, :],
                preferred_element_type=jnp.float32,
            )
            attended = term if attended is None else attended + term
        inverse = lax.rsqrt(jnp.mean(attended * attended, axis=-1, keepdims=True) + EPSILON)
        out_ref[s * SPAN : (s + 1) * SPAN, :] = (attended * inverse).astype(jnp.bfloat16)


def combine(lambda_head, messages):
    vmem = pl.BlockSpec(memory_space=pltpu.VMEM)
    return pl.pallas_call(
        combine_kernel,
        out_shape=jax.ShapeDtypeStruct((QROWS, 2 * HD), jnp.bfloat16),
        in_specs=[pl.BlockSpec(memory_space=pltpu.SMEM)] + [vmem] * NY,
        out_specs=vmem,
        compiler_params=pltpu.CompilerParams(vmem_limit_bytes=VMEM_LIMIT),
        cost_estimate=pl.CostEstimate(
            flops=1 << 27, bytes_accessed=3 << 20, transcendentals=1 << 13
        ),
        name="combine",
    )(lambda_head, *messages)


def on_device(
    queries, nbr_shard, nbr_row, database, key_weight, value_weight, lambda_head, out_weight
):
    y, z = lax.axis_index("y"), lax.axis_index("z")
    x, c = lax.axis_index("x"), lax.axis_index("c")

    entry = (nbr_shard * ENTRIES + nbr_row).astype(jnp.bfloat16).reshape(1, -1)
    entry = jnp.pad(entry, ((0, 15), (0, 2 * HD - entry.shape[1])))
    packed = jnp.concatenate([queries, entry], axis=0)
    asked = [packed] + [shift(packed, "y", k) for k in (1, 2, -1)]

    feature = jnp.concatenate(
        [
            (((x + NX - jnp.arange(NX)) % NX) * NC + side).astype(jnp.int32)
            for side in (c, 1 - c)
        ]
    )
    table = []
    for chunk in range(CHUNKS):
        tokens = database[chunk * EPC : (chunk + 1) * EPC].reshape(ROWS, -1)
        own = ring_pieces(tokens, "x")
        other = [(k, r, shift(a, "c", 1)) for k, r, a in own]
        blocks = [[a for k, _, a in side if k == d] for side in (own, other) for d in range(NX)]
        rows = project(feature, blocks, key_weight, value_weight)
        table += [
            ((chunk * NZ + k) * ROWS + r, a) for k, r, a in ring_pieces(rows, "z")
        ]

    wanted = jnp.stack([a[QROWS, : 2 * SPANS_DEV] for a in asked]).astype(jnp.int32).reshape(-1)
    shard, row = wanted // ENTRIES, wanted % ENTRIES
    active = (shard // NZ == y).astype(jnp.int32)
    offset = (
        ((row // EPC) * NZ + (z + NZ - shard % NZ) % NZ) * ROWS + (row % EPC) * NLEN
    ).astype(jnp.int32)
    outs = attend(offset, active, asked, table)
    messages = [outs[0]] + [shift(a, "y", -k) for a, k in zip(outs[1:], (1, 2, -1))]
    heads_out = combine(lambda_head, messages)

    halves = heads_out.reshape(NX, NC, SPAN, 2 * HD)
    mine = lax.dynamic_index_in_dim(halves, c, axis=1, keepdims=False)
    theirs = lax.dynamic_index_in_dim(halves, 1 - c, axis=1, keepdims=False)
    pair = jnp.concatenate([mine, shift(theirs, "c", 1)], axis=-1)
    weight = jnp.concatenate([out_weight, shift(out_weight, "c", 1)], axis=0)

    def term(k):
        rows = lax.dynamic_index_in_dim(pair, (x + k) % NX, axis=0, keepdims=False)
        return jnp.dot(rows, weight, preferred_element_type=jnp.float32)

    def add(a, b):
        return (a.astype(jnp.float32) + b).astype(jnp.bfloat16)

    half = SPAN // 2
    far = term(2).astype(jnp.bfloat16)
    up, down = shift(far[:half], "x", 1), shift(far[half:], "x", -1)
    near = term(1)
    up = jnp.concatenate([add(up, near[:half]), near[half:].astype(jnp.bfloat16)], axis=0)
    near = term(3)
    down = jnp.concatenate([near[:half].astype(jnp.bfloat16), add(down, near[half:])], axis=0)
    up, down = shift(up, "x", 1), shift(down, "x", -1)
    return (term(0) + up.astype(jnp.float32) + down.astype(jnp.float32)).astype(jnp.bfloat16)


def solution(mesh):
    fine = Mesh(mesh.devices.reshape(NY, NZ, NX, NC), ("y", "z", "x", "c"))
    db, tp = ("y", "z"), ("x", "c")
    return jax.shard_map(
        on_device,
        mesh=fine,
        in_specs=(
            P(db, tp),
            P(db, None),
            P(db, None),
            P(db, None, tp),
            P(None, tp),
            P(None, tp),
            P(tp),
            P(tp, None),
        ),
        out_specs=P(db + tp, None),
        check_vma=False,
    )
```

```python
import functools
import jax
import jax.numpy as jnp
from jax import lax
from jax.experimental import pallas as pl
from jax.experimental.pallas import tpu as pltpu
from jax.sharding import Mesh, PartitionSpec as P

HD = 128
SPAN = 64
NLEN = 128
EPSILON = 1e-05
FAR = -1e30
NY, NZ, NX, NC = 4, 8, 4, 2
SPANS_DEV = 8
ENTRIES = 4
PAIRS = ENTRIES // 2
BLOCK = 4 * NLEN
QROWS = SPANS_DEV * SPAN
WIDE = 2 * HD
OROWS = SPANS_DEV * WIDE
VMEM_LIMIT = 48 * 1024 * 1024


def shift(a, axis, k):
    n = lax.axis_size(axis)
    return lax.ppermute(a, axis, [(i, (i + k) % n) for i in range(n)])


def ring_pieces(a, axis):
    n = lax.axis_size(axis)
    half = a.shape[0] // 2
    out = [(0, 0, a)]
    up = down = a
    for k in range(1, (n - 1) // 2 + 1):
        up, down = shift(up, axis, 1), shift(down, axis, -1)
        out += [(k, 0, up), (n - k, 0, down)]
    out += [(n // 2, 0, shift(up[:half], axis, 1)), (n // 2, half, shift(down[half:], axis, -1))]
    return out


def project_kernel(layout, feature_ref, *refs):
    pieces, (key_ref, value_ref) = refs[: -2 - PAIRS], refs[-2 - PAIRS : -PAIRS]
    out_refs = refs[-PAIRS:]
    key_sum = value_sum = squares = None
    for block, members in enumerate(layout):
        rows = [pieces[i][...] for i in members]
        tokens = rows[0] if len(rows) == 1 else jnp.concatenate(rows, axis=0)
        width = tokens.shape[1]
        at = pl.ds(pl.multiple_of(feature_ref[block] * width, width), width)
        k = jnp.dot(tokens, key_ref[at, :], preferred_element_type=jnp.float32)
        v = jnp.dot(tokens, value_ref[at, :], preferred_element_type=jnp.float32)
        f = tokens.astype(jnp.float32)
        s = jnp.sum(f * f, axis=1, keepdims=True)
        if key_sum is None:
            key_sum, value_sum, squares = k, v, s
        else:
            key_sum, value_sum, squares = key_sum + k, value_sum + v, squares + s
    inverse = lax.rsqrt(squares / key_ref.shape[0] + EPSILON)
    keys = (key_sum * inverse).astype(jnp.bfloat16)
    values = value_sum * inverse
    for pair, out_ref in enumerate(out_refs):
        rows = slice(pair * 2 * NLEN, (pair + 1) * 2 * NLEN)
        out_ref[: 2 * NLEN, :] = keys[rows]
        out_ref[2 * NLEN :, :] = values[rows].T.astype(jnp.bfloat16)


def project(feature, blocks, key_weight, value_weight):
    pieces, layout = [], []
    for members in blocks:
        layout.append(tuple(range(len(pieces), len(pieces) + len(members))))
        pieces += members
    vmem = pl.BlockSpec(memory_space=pltpu.VMEM)
    return pl.pallas_call(
        functools.partial(project_kernel, tuple(layout)),
        out_shape=[jax.ShapeDtypeStruct((BLOCK, WIDE), jnp.bfloat16)] * PAIRS,
        in_specs=[pl.BlockSpec(memory_space=pltpu.SMEM)] + [vmem] * (len(pieces) + 2),
        out_specs=[vmem] * PAIRS,
        compiler_params=pltpu.CompilerParams(vmem_limit_bytes=VMEM_LIMIT),
        cost_estimate=pl.CostEstimate(
            flops=2 * 512 * 4096 * 512, bytes_accessed=8 << 20, transcendentals=0
        ),
        name="project",
    )(feature, *pieces, key_weight, value_weight)


def attend_kernel(places, place_ref, lane_ref, bias_ref, query_ref, *refs):
    pieces = refs[: len(places)]
    out_ref, table, stats, sems = refs[len(places) :]
    copies = [
        pltpu.make_async_copy(piece, table.at[pl.ds(row, piece.shape[0])], sems.at[i])
        for i, (row, piece) in enumerate(zip(places, pieces))
    ]
    for copy in copies:
        copy.start()
    lane = lax.broadcasted_iota(jnp.int32, (SPAN, WIDE), 1)
    for copy in copies:
        copy.wait()
    group = 4
    for first in range(0, SPANS_DEV, group):
        scores, values = [], []
        for s in range(first, first + group):
            block = [pl.multiple_of(place_ref[2 * s + j], BLOCK) for j in range(2)]
            side = [pl.multiple_of(lane_ref[2 * s + j], NLEN) for j in range(2)]
            keys = [table[pl.ds(block[j] + side[j], NLEN), :] for j in range(2)]
            values.append(
                jnp.concatenate(
                    [
                        table[pl.ds(block[j] + 2 * NLEN, WIDE), pl.ds(side[j], NLEN)]
                        for j in range(2)
                    ],
                    axis=1,
                )
            )
            q = query_ref[s * SPAN : (s + 1) * SPAN, :]
            zero = jnp.zeros_like(q)
            both = jnp.concatenate(
                [jnp.where(lane < HD, q, zero), jnp.where(lane >= HD, q, zero)], axis=0
            )
            products = lax.dot_general(
                jnp.concatenate(keys, axis=0),
                both,
                (((1,), (1,)), ((), ())),
                preferred_element_type=jnp.float32,
            ) * (1.0 / HD**0.5)
            scores.append([products[j * NLEN : (j + 1) * NLEN] + bias_ref[2 * s + j] for j in range(2)])
        shares, levels = [], []
        for one, two in scores:
            top = jnp.max(jnp.maximum(one, two), axis=0, keepdims=True)
            one, two = jnp.exp(one - top), jnp.exp(two - top)
            total = jnp.sum(one + two, axis=0, keepdims=True)
            levels.append(top + jnp.log(total))
            inverse = 1.0 / total
            shares.append(
                jnp.concatenate([one * inverse, two * inverse], axis=0).astype(jnp.bfloat16)
            )
        attended = [
            jnp.dot(v, p, preferred_element_type=jnp.float32).astype(jnp.bfloat16)
            for v, p in zip(values, shares)
        ]
        for i, s in enumerate(range(first, first + group)):
            out_ref[s * WIDE : (s + 1) * WIDE, :] = attended[i]
            stats[s : s + 1, :] = levels[i]
    level = stats[...]
    high = level.astype(jnp.bfloat16).astype(jnp.float32)
    rest = level - high
    mid = rest.astype(jnp.bfloat16).astype(jnp.float32)
    low = rest - mid
    coded = jnp.concatenate([high, mid, low, jnp.zeros_like(low)], axis=0)
    out_ref[OROWS:, :] = coded.astype(jnp.bfloat16)


def attend(place, lane, bias, queries, pieces):
    places = tuple(row for row, _ in pieces)
    smem = pl.BlockSpec(memory_space=pltpu.SMEM)
    vmem = pl.BlockSpec(memory_space=pltpu.VMEM)
    return pl.pallas_call(
        functools.partial(attend_kernel, places),
        out_shape=jax.ShapeDtypeStruct((OROWS + 4 * SPANS_DEV, 2 * SPAN), jnp.bfloat16),
        in_specs=[smem] * 3 + [vmem] + [pl.BlockSpec(memory_space=pltpu.HBM)] * len(pieces),
        out_specs=vmem,
        scratch_shapes=[
            pltpu.VMEM((PAIRS * NZ * BLOCK, WIDE), jnp.bfloat16),
            pltpu.VMEM((SPANS_DEV, 2 * SPAN), jnp.float32),
            pltpu.SemaphoreType.DMA((len(pieces),)),
        ],
        compiler_params=pltpu.CompilerParams(vmem_limit_bytes=VMEM_LIMIT),
        cost_estimate=pl.CostEstimate(
            flops=1 << 29, bytes_accessed=6 << 20, transcendentals=1 << 18
        ),
        name="attend",
    )(place, lane, bias, queries, *[a for _, a in pieces])


def combine_kernel(lambda_ref, *refs):
    *messages, out_ref = refs
    levels = []
    for message in messages:
        coded = message[OROWS:, :].astype(jnp.float32)
        n = SPANS_DEV
        levels.append((coded[:n] + coded[n : 2 * n]) + coded[2 * n : 3 * n])
    top = functools.reduce(jnp.maximum, levels)
    parts = [jnp.exp(level - top) for level in levels]
    total = functools.reduce(jnp.add, parts)
    lane = lax.broadcasted_iota(jnp.int32, (SPANS_DEV, 2 * SPAN), 1)
    sign = jnp.where(lane < SPAN, 1.0, -lambda_ref[0])
    factors = [part * (sign / total) for part in parts]
    first = lax.broadcasted_iota(jnp.int32, (WIDE, 2 * SPAN), 1) < SPAN
    for pair in range(SPANS_DEV // 2):
        both = []
        for s in (2 * pair, 2 * pair + 1):
            maps = functools.reduce(
                jnp.add,
                [
                    message[s * WIDE : (s + 1) * WIDE, :].astype(jnp.float32) * factor[s : s + 1, :]
                    for factor, message in zip(factors, messages)
                ],
            )
            both.append(maps + pltpu.roll(maps, SPAN, 1))
        attended = jnp.where(first, both[0], both[1])
        inverse = lax.rsqrt(jnp.mean(attended * attended, axis=0, keepdims=True) + EPSILON)
        out_ref[2 * pair * SPAN : 2 * (pair + 1) * SPAN, :] = (attended * inverse).T.astype(
            jnp.bfloat16
        )


def combine(lambda_head, messages):
    vmem = pl.BlockSpec(memory_space=pltpu.VMEM)
    return pl.pallas_call(
        combine_kernel,
        out_shape=jax.ShapeDtypeStruct((QROWS, WIDE), jnp.bfloat16),
        in_specs=[pl.BlockSpec(memory_space=pltpu.SMEM)] + [vmem] * NY,
        out_specs=vmem,
        compiler_params=pltpu.CompilerParams(vmem_limit_bytes=VMEM_LIMIT),
        cost_estimate=pl.CostEstimate(
            flops=1 << 23, bytes_accessed=3 << 20, transcendentals=1 << 13
        ),
        name="combine",
    )(lambda_head, *messages)


def on_device(
    queries, nbr_shard, nbr_row, database, key_weight, value_weight, lambda_head, out_weight
):
    y, z = lax.axis_index("y"), lax.axis_index("z")
    x, c = lax.axis_index("x"), lax.axis_index("c")

    entry = (nbr_shard * ENTRIES + nbr_row).astype(jnp.bfloat16).reshape(1, -1)
    entry = jnp.pad(entry, ((0, 15), (0, 2 * HD - entry.shape[1])))
    packed = jnp.concatenate([queries, entry], axis=0)
    asked = [packed] + [shift(packed, "y", k) for k in (1, 2, -1)]

    feature = jnp.concatenate(
        [
            (((x + NX - jnp.arange(NX)) % NX) * NC + side).astype(jnp.int32)
            for side in (c, 1 - c)
        ]
    )
    own = ring_pieces(database.reshape(ENTRIES * NLEN, -1), "x")
    other = [(k, r, shift(a, "c", 1)) for k, r, a in own]
    blocks = [[a for k, _, a in side if k == d] for side in (own, other) for d in range(NX)]
    rows = project(feature, blocks, key_weight, value_weight)
    table = [
        ((pair * NZ + k) * BLOCK + r, a)
        for pair in range(PAIRS)
        for k, r, a in ring_pieces(rows[pair], "z")
    ]

    held_back, _ = lax.optimization_barrier((out_weight, rows[0]))
    weight = lax.all_gather(held_back, ("x", "c"), axis=0, tiled=True)

    wanted = jnp.stack([a[QROWS, : 2 * SPANS_DEV] for a in asked]).astype(jnp.int32)
    shard, row = wanted // ENTRIES, wanted % ENTRIES
    bias = jnp.where(shard // NZ == y, 0.0, FAR).astype(jnp.float32)
    place = (((row // 2) * NZ + (z + NZ - shard % NZ) % NZ) * BLOCK).astype(jnp.int32)
    lane = ((row % 2) * NLEN).astype(jnp.int32)
    messages = [None] * NY
    for k in (2, 1, 3, 0):
        out = attend(place[k], lane[k], bias[k], asked[k], table)
        messages[k] = shift(out, "y", -k) if k else out
    heads_out = combine(lambda_head, messages)

    heads = lax.all_to_all(
        heads_out.reshape(NX * NC, SPAN, WIDE), ("x", "c"), split_axis=0, concat_axis=0, tiled=True
    )
    rows = jnp.swapaxes(heads, 0, 1).reshape(SPAN, NX * NC * WIDE)
    return jnp.dot(rows, weight, preferred_element_type=jnp.float32).astype(jnp.bfloat16)


def solution(mesh):
    fine = Mesh(mesh.devices.reshape(NY, NZ, NX, NC), ("y", "z", "x", "c"))
    db, tp = ("y", "z"), ("x", "c")
    return jax.shard_map(
        on_device,
        mesh=fine,
        in_specs=(
            P(db, tp),
            P(db, None),
            P(db, None),
            P(db, None, tp),
            P(None, tp),
            P(None, tp),
            P(tp),
            P(tp, None),
        ),
        out_specs=P(db + tp, None),
        check_vma=False,
    )
```

```python
import functools
import jax
import jax.numpy as jnp
from jax import lax
from jax.experimental import pallas as pl
from jax.experimental.pallas import tpu as pltpu
from jax.sharding import Mesh, PartitionSpec as P

HD = 128
SPAN = 64
NLEN = 128
EPSILON = 1e-05
FAR = -1e30
NY, NZ, NX, NC = 4, 8, 4, 2
SPANS_DEV = 8
ENTRIES = 4
PAIRS = ENTRIES // 2
BLOCK = 4 * NLEN
QROWS = SPANS_DEV * SPAN
WIDE = 2 * HD
OROWS = SPANS_DEV * WIDE
VMEM_LIMIT = 48 * 1024 * 1024
PROJECT_LIMIT = 58 * 1024 * 1024


def shift(a, axis, k):
    n = lax.axis_size(axis)
    return lax.ppermute(a, axis, [(i, (i + k) % n) for i in range(n)])


def ring_pieces(a, axis):
    n = lax.axis_size(axis)
    half = a.shape[0] // 2
    out = [(0, 0, a)]
    up = down = a
    for k in range(1, (n - 1) // 2 + 1):
        up, down = shift(up, axis, 1), shift(down, axis, -1)
        out += [(k, 0, up), (n - k, 0, down)]
    out += [(n // 2, 0, shift(up[:half], axis, 1)), (n // 2, half, shift(down[half:], axis, -1))]
    return out


def project_kernel(rows, feature_ref, *refs):
    n = len(rows)
    pieces, (key_ref, value_ref, out_ref, tokens, weights, sems) = refs[:n], refs[n:]
    width = tokens.shape[2]
    copies = []
    for i, (row, piece) in enumerate(zip(rows, pieces)):
        at = pl.ds(pl.multiple_of(feature_ref[i] * width, width), width)
        copies.append(
            [
                pltpu.make_async_copy(piece.at[pl.ds(row, 2 * NLEN)], tokens.at[i], sems.at[i]),
                pltpu.make_async_copy(key_ref.at[at], weights.at[i], sems.at[n + i]),
                pltpu.make_async_copy(value_ref.at[at], weights.at[n + i], sems.at[2 * n + i]),
            ]
        )
    for group in copies:
        for copy in group:
            copy.start()
    key_sum = value_sum = squares = None
    for i, group in enumerate(copies):
        for copy in group:
            copy.wait()
        block = tokens[i]
        k = jnp.dot(block, weights[i], preferred_element_type=jnp.float32)
        v = jnp.dot(block, weights[n + i], preferred_element_type=jnp.float32)
        f = block.astype(jnp.float32)
        s = jnp.sum(f * f, axis=1, keepdims=True)
        if key_sum is None:
            key_sum, value_sum, squares = k, v, s
        else:
            key_sum, value_sum, squares = key_sum + k, value_sum + v, squares + s
    inverse = lax.rsqrt(squares / key_ref.shape[0] + EPSILON)
    out_ref[: 2 * NLEN, :] = (key_sum * inverse).astype(jnp.bfloat16)
    out_ref[2 * NLEN :, :] = (value_sum * inverse).T.astype(jnp.bfloat16)


def project(feature, blocks, key_weight, value_weight):
    rows = tuple(row for row, _ in blocks)
    width = key_weight.shape[0] // len(blocks)
    vmem = pl.BlockSpec(memory_space=pltpu.VMEM)
    return pl.pallas_call(
        functools.partial(project_kernel, rows),
        out_shape=jax.ShapeDtypeStruct((BLOCK, WIDE), jnp.bfloat16),
        in_specs=[pl.BlockSpec(memory_space=pltpu.SMEM)]
        + [pl.BlockSpec(memory_space=pltpu.HBM)] * (len(blocks) + 2),
        out_specs=vmem,
        scratch_shapes=[
            pltpu.VMEM((len(blocks), 2 * NLEN, width), jnp.bfloat16),
            pltpu.VMEM((2 * len(blocks), width, WIDE), jnp.bfloat16),
            pltpu.SemaphoreType.DMA((3 * len(blocks),)),
        ],
        compiler_params=pltpu.CompilerParams(vmem_limit_bytes=PROJECT_LIMIT),
        cost_estimate=pl.CostEstimate(
            flops=256 * 4096 * 1024, bytes_accessed=6 << 20, transcendentals=0
        ),
        name="project",
    )(feature, *[a for _, a in blocks], key_weight, value_weight)


def attend_kernel(places, place_ref, lane_ref, bias_ref, query_ref, *refs):
    pieces = refs[: len(places)]
    out_ref, table, stats, sems = refs[len(places) :]
    copies = [
        pltpu.make_async_copy(piece, table.at[pl.ds(row, piece.shape[0])], sems.at[i])
        for i, (row, piece) in enumerate(zip(places, pieces))
    ]
    for copy in copies:
        copy.start()
    lane = lax.broadcasted_iota(jnp.int32, (SPAN, WIDE), 1)
    for copy in copies:
        copy.wait()
    group = 4
    for first in range(0, SPANS_DEV, group):
        scores, values = [], []
        for s in range(first, first + group):
            block = [pl.multiple_of(place_ref[2 * s + j], BLOCK) for j in range(2)]
            side = [pl.multiple_of(lane_ref[2 * s + j], NLEN) for j in range(2)]
            keys = [table[pl.ds(block[j] + side[j], NLEN), :] for j in range(2)]
            values.append(
                jnp.concatenate(
                    [
                        table[pl.ds(block[j] + 2 * NLEN, WIDE), pl.ds(side[j], NLEN)]
                        for j in range(2)
                    ],
                    axis=1,
                )
            )
            q = query_ref[s * SPAN : (s + 1) * SPAN, :]
            zero = jnp.zeros_like(q)
            both = jnp.concatenate(
                [jnp.where(lane < HD, q, zero), jnp.where(lane >= HD, q, zero)], axis=0
            )
            products = lax.dot_general(
                jnp.concatenate(keys, axis=0),
                both,
                (((1,), (1,)), ((), ())),
                preferred_element_type=jnp.float32,
            ) * (1.0 / HD**0.5)
            scores.append([products[j * NLEN : (j + 1) * NLEN] + bias_ref[2 * s + j] for j in range(2)])
        shares, levels = [], []
        for one, two in scores:
            top = jnp.max(jnp.maximum(one, two), axis=0, keepdims=True)
            one, two = jnp.exp(one - top), jnp.exp(two - top)
            total = jnp.sum(one + two, axis=0, keepdims=True)
            levels.append(top + jnp.log(total))
            inverse = 1.0 / total
            shares.append(
                jnp.concatenate([one * inverse, two * inverse], axis=0).astype(jnp.bfloat16)
            )
        attended = [
            jnp.dot(v, p, preferred_element_type=jnp.float32).astype(jnp.bfloat16)
            for v, p in zip(values, shares)
        ]
        for i, s in enumerate(range(first, first + group)):
            out_ref[s * WIDE : (s + 1) * WIDE, :] = attended[i]
            stats[s : s + 1, :] = levels[i]
    level = stats[...]
    high = level.astype(jnp.bfloat16).astype(jnp.float32)
    rest = level - high
    mid = rest.astype(jnp.bfloat16).astype(jnp.float32)
    low = rest - mid
    coded = jnp.concatenate([high, mid, low, jnp.zeros_like(low)], axis=0)
    out_ref[OROWS:, :] = coded.astype(jnp.bfloat16)


def attend(place, lane, bias, queries, pieces):
    places = tuple(row for row, _ in pieces)
    smem = pl.BlockSpec(memory_space=pltpu.SMEM)
    vmem = pl.BlockSpec(memory_space=pltpu.VMEM)
    return pl.pallas_call(
        functools.partial(attend_kernel, places),
        out_shape=jax.ShapeDtypeStruct((OROWS + 4 * SPANS_DEV, 2 * SPAN), jnp.bfloat16),
        in_specs=[smem] * 3 + [vmem] + [pl.BlockSpec(memory_space=pltpu.HBM)] * len(pieces),
        out_specs=vmem,
        scratch_shapes=[
            pltpu.VMEM((PAIRS * NZ * BLOCK, WIDE), jnp.bfloat16),
            pltpu.VMEM((SPANS_DEV, 2 * SPAN), jnp.float32),
            pltpu.SemaphoreType.DMA((len(pieces),)),
        ],
        compiler_params=pltpu.CompilerParams(vmem_limit_bytes=VMEM_LIMIT),
        cost_estimate=pl.CostEstimate(
            flops=1 << 29, bytes_accessed=6 << 20, transcendentals=1 << 18
        ),
        name="attend",
    )(place, lane, bias, queries, *[a for _, a in pieces])


def combine_kernel(lambda_ref, *refs):
    *messages, out_ref = refs
    levels = []
    for message in messages:
        coded = message[OROWS:, :].astype(jnp.float32)
        n = SPANS_DEV
        levels.append((coded[:n] + coded[n : 2 * n]) + coded[2 * n : 3 * n])
    top = functools.reduce(jnp.maximum, levels)
    parts = [jnp.exp(level - top) for level in levels]
    total = functools.reduce(jnp.add, parts)
    lane = lax.broadcasted_iota(jnp.int32, (SPANS_DEV, 2 * SPAN), 1)
    sign = jnp.where(lane < SPAN, 1.0, -lambda_ref[0])
    factors = [part * (sign / total) for part in parts]
    first = lax.broadcasted_iota(jnp.int32, (WIDE, 2 * SPAN), 1) < SPAN
    for pair in range(SPANS_DEV // 2):
        both = []
        for s in (2 * pair, 2 * pair + 1):
            maps = functools.reduce(
                jnp.add,
                [
                    message[s * WIDE : (s + 1) * WIDE, :].astype(jnp.float32) * factor[s : s + 1, :]
                    for factor, message in zip(factors, messages)
                ],
            )
            both.append(maps + pltpu.roll(maps, SPAN, 1))
        attended = jnp.where(first, both[0], both[1])
        inverse = lax.rsqrt(jnp.mean(attended * attended, axis=0, keepdims=True) + EPSILON)
        out_ref[2 * pair * SPAN : 2 * (pair + 1) * SPAN, :] = (attended * inverse).T.astype(
            jnp.bfloat16
        )


def combine(lambda_head, messages):
    vmem = pl.BlockSpec(memory_space=pltpu.VMEM)
    return pl.pallas_call(
        combine_kernel,
        out_shape=jax.ShapeDtypeStruct((QROWS, WIDE), jnp.bfloat16),
        in_specs=[pl.BlockSpec(memory_space=pltpu.SMEM)] + [vmem] * NY,
        out_specs=vmem,
        compiler_params=pltpu.CompilerParams(vmem_limit_bytes=VMEM_LIMIT),
        cost_estimate=pl.CostEstimate(
            flops=1 << 23, bytes_accessed=3 << 20, transcendentals=1 << 13
        ),
        name="combine",
    )(lambda_head, *messages)


def output_kernel(rows_ref, weight_ref, out_ref):
    out_ref[...] = jnp.dot(
        rows_ref[...], weight_ref[...], preferred_element_type=jnp.float32
    ).astype(jnp.bfloat16)


def output(rows, weight):
    depth, width = weight.shape
    step = 512
    return pl.pallas_call(
        output_kernel,
        grid=(width // step,),
        out_shape=jax.ShapeDtypeStruct((rows.shape[0], width), jnp.bfloat16),
        in_specs=[
            pl.BlockSpec((rows.shape[0], depth), lambda i: (0, 0)),
            pl.BlockSpec((depth, step), lambda i: (0, i)),
        ],
        out_specs=pl.BlockSpec((rows.shape[0], step), lambda i: (0, i)),
        compiler_params=pltpu.CompilerParams(vmem_limit_bytes=VMEM_LIMIT),
        cost_estimate=pl.CostEstimate(
            flops=2 * 64 * 2048 * 4096, bytes_accessed=16 << 20, transcendentals=0
        ),
        name="output",
    )(rows, weight)


def on_device(
    queries, nbr_shard, nbr_row, database, key_weight, value_weight, lambda_head, out_weight
):
    y, z = lax.axis_index("y"), lax.axis_index("z")
    x, c = lax.axis_index("x"), lax.axis_index("c")

    entry = (nbr_shard * ENTRIES + nbr_row).astype(jnp.bfloat16).reshape(1, -1)
    entry = jnp.pad(entry, ((0, 15), (0, 2 * HD - entry.shape[1])))
    packed = jnp.concatenate([queries, entry], axis=0)
    asked = [packed] + [shift(packed, "y", k) for k in (1, 2, -1)]

    feature = jnp.concatenate(
        [
            (((x + NX - jnp.arange(NX)) % NX) * NC + side).astype(jnp.int32)
            for side in (c, 1 - c)
        ]
    )
    tokens = database.reshape(ENTRIES * NLEN, -1)
    half = tokens.shape[0] // 2
    up, down = shift(tokens, "x", 1), shift(tokens, "x", -1)
    *asked, low, high = lax.optimization_barrier((*asked, up[:half], down[half:]))
    own = [(0, 0, tokens), (1, 0, up), (3, 0, down)]
    own += [(2, 0, shift(low, "x", 1)), (2, half, shift(high, "x", -1))]
    other = [(k, r, shift(a, "c", 1)) for k, r, a in own]
    arrived = lax.optimization_barrier([a for _, _, a in own + other])
    own, other = (
        [(k, r, a) for (k, r, _), a in zip(own, arrived[at : at + len(own)])]
        for at in (0, len(own))
    )
    rows = []
    for pair in range(PAIRS):
        blocks = []
        for side in (own, other):
            for d in range(NX):
                for k, r, a in side:
                    if k == d and r <= pair * half < r + a.shape[0]:
                        blocks.append((pair * half - r, a))
        rows.append(project(feature, blocks, key_weight, value_weight))
    table = [
        ((pair * NZ + k) * BLOCK + r, a)
        for pair in range(PAIRS)
        for k, r, a in ring_pieces(rows[pair], "z")
    ]

    held_back, _ = lax.optimization_barrier((out_weight, rows[0]))
    weight = lax.all_gather(held_back, ("x", "c"), axis=0, tiled=True)

    wanted = jnp.stack([a[QROWS, : 2 * SPANS_DEV] for a in asked]).astype(jnp.int32)
    shard, row = wanted // ENTRIES, wanted % ENTRIES
    bias = jnp.where(shard // NZ == y, 0.0, FAR).astype(jnp.float32)
    place = (((row // 2) * NZ + (z + NZ - shard % NZ) % NZ) * BLOCK).astype(jnp.int32)
    lane = ((row % 2) * NLEN).astype(jnp.int32)
    messages = [None] * NY
    for k in (2, 1, 3, 0):
        out = attend(place[k], lane[k], bias[k], asked[k], table)
        messages[k] = shift(out, "y", -k) if k else out
    heads_out = combine(lambda_head, messages)

    heads = lax.all_to_all(
        heads_out.reshape(NX * NC, SPAN, WIDE), ("x", "c"), split_axis=0, concat_axis=0, tiled=True
    )
    rows = jnp.swapaxes(heads, 0, 1).reshape(SPAN, NX * NC * WIDE)
    return output(rows, weight)


def solution(mesh):
    fine = Mesh(mesh.devices.reshape(NY, NZ, NX, NC), ("y", "z", "x", "c"))
    db, tp = ("y", "z"), ("x", "c")
    return jax.shard_map(
        on_device,
        mesh=fine,
        in_specs=(
            P(db, tp),
            P(db, None),
            P(db, None),
            P(db, None, tp),
            P(None, tp),
            P(None, tp),
            P(tp),
            P(tp, None),
        ),
        out_specs=P(db + tp, None),
        check_vma=False,
    )
```

```python
import functools
import jax
import jax.numpy as jnp
from jax import lax
from jax.experimental import pallas as pl
from jax.experimental.pallas import tpu as pltpu
from jax.sharding import Mesh, PartitionSpec as P

HD = 128
SPAN = 64
NLEN = 128
EPSILON = 1e-05
FAR = -1e30
NY, NZ, NX, NC = 4, 8, 4, 2
SPANS_DEV = 8
ENTRIES = 4
PAIRS = ENTRIES // 2
BLOCK = 4 * NLEN
QROWS = SPANS_DEV * SPAN
WIDE = 2 * HD
OROWS = SPANS_DEV * WIDE
VMEM_LIMIT = 48 * 1024 * 1024


def shift(a, axis, k):
    n = lax.axis_size(axis)
    return lax.ppermute(a, axis, [(i, (i + k) % n) for i in range(n)])


def ring_pieces(a, axis):
    n = lax.axis_size(axis)
    half = a.shape[0] // 2
    out = [(0, 0, a)]
    up = down = a
    for k in range(1, (n - 1) // 2 + 1):
        up, down = shift(up, axis, 1), shift(down, axis, -1)
        out += [(k, 0, up), (n - k, 0, down)]
    out += [(n // 2, 0, shift(up[:half], axis, 1)), (n // 2, half, shift(down[half:], axis, -1))]
    return out


def add_block(sums, tokens, key_rows, value_rows):
    f = tokens.astype(jnp.float32)
    terms = (
        jnp.dot(tokens, key_rows, preferred_element_type=jnp.float32),
        jnp.dot(tokens, value_rows, preferred_element_type=jnp.float32),
        jnp.sum(f * f, axis=1, keepdims=True),
    )
    return terms if sums is None else tuple(a + b for a, b in zip(sums, terms))


def weight_copies(feature_ref, key_ref, value_ref, places, sems):
    copies = []
    for i, (key_place, value_place) in enumerate(places):
        width = key_place.shape[0]
        at = pl.ds(pl.multiple_of(feature_ref[i] * width, width), width)
        copies.append(
            [
                pltpu.make_async_copy(key_ref.at[at], key_place, sems.at[2 * i]),
                pltpu.make_async_copy(value_ref.at[at], value_place, sems.at[2 * i + 1]),
            ]
        )
    for group in copies:
        for copy in group:
            copy.start()
    return copies


def early_kernel(feature_ref, *refs):
    pieces, rest = refs[:-7], refs[-7:]
    key_ref, value_ref, sum_ref, square_ref, late_ref, weights, sems = rest
    places = [(weights.at[2 * i], weights.at[2 * i + 1]) for i in range(len(pieces))]
    places += [(late_ref.at[2 * i], late_ref.at[2 * i + 1]) for i in range(late_ref.shape[0] // 2)]
    copies = weight_copies(feature_ref, key_ref, value_ref, places, sems)
    sums = None
    for i, piece in enumerate(pieces):
        for copy in copies[i]:
            copy.wait()
        sums = add_block(sums, piece[...], weights[2 * i], weights[2 * i + 1])
    sum_ref[:, :WIDE] = sums[0]
    sum_ref[:, WIDE:] = sums[1]
    square_ref[...] = jnp.broadcast_to(sums[2], square_ref.shape)
    for group in copies[len(pieces) :]:
        for copy in group:
            copy.wait()


def late_kernel(depth, *refs):
    *pieces, sum_ref, square_ref, weights, out_0, out_1 = refs
    for pair, out_ref in enumerate((out_0, out_1)):
        rows = slice(pair * 2 * NLEN, (pair + 1) * 2 * NLEN)
        sums = (sum_ref[rows, :WIDE], sum_ref[rows, WIDE:], square_ref[rows, :1])
        for i in range(len(pieces) // PAIRS):
            sums = add_block(
                sums, pieces[i * PAIRS + pair][...], weights[2 * i], weights[2 * i + 1]
            )
        inverse = lax.rsqrt(sums[2] / depth + EPSILON)
        out_ref[: 2 * NLEN, :] = (sums[0] * inverse).astype(jnp.bfloat16)
        out_ref[2 * NLEN :, :] = (sums[1] * inverse).T.astype(jnp.bfloat16)


def project_early(feature, pieces, key_weight, value_weight):
    tokens, width = pieces[0].shape
    blocks, count = feature.shape[0], len(pieces)
    vmem = pl.BlockSpec(memory_space=pltpu.VMEM)
    return pl.pallas_call(
        early_kernel,
        out_shape=[
            jax.ShapeDtypeStruct((tokens, 2 * WIDE), jnp.float32),
            jax.ShapeDtypeStruct((tokens, HD), jnp.float32),
            jax.ShapeDtypeStruct((2 * (blocks - count), width, WIDE), jnp.bfloat16),
        ],
        in_specs=[pl.BlockSpec(memory_space=pltpu.SMEM)]
        + [vmem] * count
        + [pl.BlockSpec(memory_space=pltpu.HBM)] * 2,
        out_specs=[vmem] * 3,
        scratch_shapes=[
            pltpu.VMEM((2 * count, width, WIDE), jnp.bfloat16),
            pltpu.SemaphoreType.DMA((2 * blocks,)),
        ],
        compiler_params=pltpu.CompilerParams(vmem_limit_bytes=VMEM_LIMIT),
        cost_estimate=pl.CostEstimate(
            flops=count * 512 * 512 * 1024, bytes_accessed=count << 20, transcendentals=0
        ),
        name="project_early",
    )(feature, *pieces, key_weight, value_weight)


def project_late(pieces, sums, depth):
    vmem = pl.BlockSpec(memory_space=pltpu.VMEM)
    return pl.pallas_call(
        functools.partial(late_kernel, depth),
        out_shape=[jax.ShapeDtypeStruct((BLOCK, WIDE), jnp.bfloat16)] * PAIRS,
        in_specs=[vmem] * (len(pieces) + len(sums)),
        out_specs=[vmem] * PAIRS,
        compiler_params=pltpu.CompilerParams(vmem_limit_bytes=VMEM_LIMIT),
        cost_estimate=pl.CostEstimate(
            flops=2 * 512 * 512 * 1024, bytes_accessed=2 << 20, transcendentals=0
        ),
        name="project_late",
    )(*pieces, *sums)


def attend_kernel(places, place_ref, lane_ref, bias_ref, query_ref, *refs):
    pieces = refs[: len(places)]
    out_ref, table, stats, sems = refs[len(places) :]
    copies = [
        pltpu.make_async_copy(piece, table.at[pl.ds(row, piece.shape[0])], sems.at[i])
        for i, (row, piece) in enumerate(zip(places, pieces))
    ]
    for copy in copies:
        copy.start()
    lane = lax.broadcasted_iota(jnp.int32, (SPAN, WIDE), 1)
    for copy in copies:
        copy.wait()
    group = 4
    for first in range(0, SPANS_DEV, group):
        scores, values = [], []
        for s in range(first, first + group):
            block = [pl.multiple_of(place_ref[2 * s + j], BLOCK) for j in range(2)]
            side = [pl.multiple_of(lane_ref[2 * s + j], NLEN) for j in range(2)]
            keys = [table[pl.ds(block[j] + side[j], NLEN), :] for j in range(2)]
            values.append(
                jnp.concatenate(
                    [
                        table[pl.ds(block[j] + 2 * NLEN, WIDE), pl.ds(side[j], NLEN)]
                        for j in range(2)
                    ],
                    axis=1,
                )
            )
            q = query_ref[s * SPAN : (s + 1) * SPAN, :]
            zero = jnp.zeros_like(q)
            both = jnp.concatenate(
                [jnp.where(lane < HD, q, zero), jnp.where(lane >= HD, q, zero)], axis=0
            )
            products = lax.dot_general(
                jnp.concatenate(keys, axis=0),
                both,
                (((1,), (1,)), ((), ())),
                preferred_element_type=jnp.float32,
            ) * (1.0 / HD**0.5)
            scores.append([products[j * NLEN : (j + 1) * NLEN] + bias_ref[2 * s + j] for j in range(2)])
        shares, levels = [], []
        for one, two in scores:
            top = jnp.max(jnp.maximum(one, two), axis=0, keepdims=True)
            one, two = jnp.exp(one - top), jnp.exp(two - top)
            total = jnp.sum(one + two, axis=0, keepdims=True)
            levels.append(top + jnp.log(total))
            inverse = 1.0 / total
            shares.append(
                jnp.concatenate([one * inverse, two * inverse], axis=0).astype(jnp.bfloat16)
            )
        attended = [
            jnp.dot(v, p, preferred_element_type=jnp.float32).astype(jnp.bfloat16)
            for v, p in zip(values, shares)
        ]
        for i, s in enumerate(range(first, first + group)):
            out_ref[s * WIDE : (s + 1) * WIDE, :] = attended[i]
            stats[s : s + 1, :] = levels[i]
    level = stats[...]
    high = level.astype(jnp.bfloat16).astype(jnp.float32)
    rest = level - high
    mid = rest.astype(jnp.bfloat16).astype(jnp.float32)
    low = rest - mid
    coded = jnp.concatenate([high, mid, low, jnp.zeros_like(low)], axis=0)
    out_ref[OROWS:, :] = coded.astype(jnp.bfloat16)


def attend(place, lane, bias, queries, pieces):
    places = tuple(row for row, _ in pieces)
    smem = pl.BlockSpec(memory_space=pltpu.SMEM)
    vmem = pl.BlockSpec(memory_space=pltpu.VMEM)
    return pl.pallas_call(
        functools.partial(attend_kernel, places),
        out_shape=jax.ShapeDtypeStruct((OROWS + 4 * SPANS_DEV, 2 * SPAN), jnp.bfloat16),
        in_specs=[smem] * 3 + [vmem] + [pl.BlockSpec(memory_space=pltpu.HBM)] * len(pieces),
        out_specs=vmem,
        scratch_shapes=[
            pltpu.VMEM((PAIRS * NZ * BLOCK, WIDE), jnp.bfloat16),
            pltpu.VMEM((SPANS_DEV, 2 * SPAN), jnp.float32),
            pltpu.SemaphoreType.DMA((len(pieces),)),
        ],
        compiler_params=pltpu.CompilerParams(vmem_limit_bytes=VMEM_LIMIT),
        cost_estimate=pl.CostEstimate(
            flops=1 << 29, bytes_accessed=6 << 20, transcendentals=1 << 18
        ),
        name="attend",
    )(place, lane, bias, queries, *[a for _, a in pieces])


def combine_kernel(lambda_ref, *refs):
    *messages, out_ref = refs
    levels = []
    for message in messages:
        coded = message[OROWS:, :].astype(jnp.float32)
        n = SPANS_DEV
        levels.append((coded[:n] + coded[n : 2 * n]) + coded[2 * n : 3 * n])
    top = functools.reduce(jnp.maximum, levels)
    parts = [jnp.exp(level - top) for level in levels]
    total = functools.reduce(jnp.add, parts)
    lane = lax.broadcasted_iota(jnp.int32, (SPANS_DEV, 2 * SPAN), 1)
    sign = jnp.where(lane < SPAN, 1.0, -lambda_ref[0])
    factors = [part * (sign / total) for part in parts]
    first = lax.broadcasted_iota(jnp.int32, (WIDE, 2 * SPAN), 1) < SPAN
    for pair in range(SPANS_DEV // 2):
        both = []
        for s in (2 * pair, 2 * pair + 1):
            maps = functools.reduce(
                jnp.add,
                [
                    message[s * WIDE : (s + 1) * WIDE, :].astype(jnp.float32) * factor[s : s + 1, :]
                    for factor, message in zip(factors, messages)
                ],
            )
            both.append(maps + pltpu.roll(maps, SPAN, 1))
        attended = jnp.where(first, both[0], both[1])
        inverse = lax.rsqrt(jnp.mean(attended * attended, axis=0, keepdims=True) + EPSILON)
        out_ref[2 * pair * SPAN : 2 * (pair + 1) * SPAN, :] = (attended * inverse).T.astype(
            jnp.bfloat16
        )


def combine(lambda_head, messages):
    vmem = pl.BlockSpec(memory_space=pltpu.VMEM)
    return pl.pallas_call(
        combine_kernel,
        out_shape=jax.ShapeDtypeStruct((QROWS, WIDE), jnp.bfloat16),
        in_specs=[pl.BlockSpec(memory_space=pltpu.SMEM)] + [vmem] * NY,
        out_specs=vmem,
        compiler_params=pltpu.CompilerParams(vmem_limit_bytes=VMEM_LIMIT),
        cost_estimate=pl.CostEstimate(
            flops=1 << 23, bytes_accessed=3 << 20, transcendentals=1 << 13
        ),
        name="combine",
    )(lambda_head, *messages)


def on_device(
    queries, nbr_shard, nbr_row, database, key_weight, value_weight, lambda_head, out_weight
):
    y, z = lax.axis_index("y"), lax.axis_index("z")
    x, c = lax.axis_index("x"), lax.axis_index("c")

    def feature(*offsets):
        return jnp.stack(
            [((x + NX - k) % NX) * NC + side for k in offsets for side in (c, 1 - c)]
        ).astype(jnp.int32)

    tokens = database.reshape(ENTRIES * NLEN, -1)
    half = tokens.shape[0] // 2
    up, down = shift(tokens, "x", 1), shift(tokens, "x", -1)
    low, high = shift(up[:half], "x", 1), shift(down[half:], "x", -1)
    early = [p for a in (tokens, up, down) for p in (a, shift(a, "c", 1))]
    sums = project_early(feature(0, 1, 3, 2), early, key_weight, value_weight)
    low, high, *sums = lax.optimization_barrier((low, high, *sums))
    late = [low, high, shift(low, "c", 1), shift(high, "c", 1)]
    rows = project_late(late, sums, key_weight.shape[0])
    table = [
        ((pair * NZ + k) * BLOCK + r, a)
        for pair in range(PAIRS)
        for k, r, a in ring_pieces(rows[pair], "z")
    ]

    entry = (nbr_shard * ENTRIES + nbr_row).astype(jnp.bfloat16).reshape(1, -1)
    entry = jnp.pad(entry, ((0, 15), (0, WIDE - entry.shape[1])))
    packed = jnp.concatenate([queries, entry], axis=0)
    asked = [packed]
    for k, place in ((1, 1), (2, 2), (-1, 3)):
        after, _ = lax.optimization_barrier((packed, table[place][1]))
        asked.append(shift(after, "y", k))

    held_back, _ = lax.optimization_barrier((out_weight, rows[0]))
    weight = lax.all_gather(held_back, ("x", "c"), axis=0, tiled=True)

    wanted = jnp.stack([a[QROWS, : 2 * SPANS_DEV] for a in asked]).astype(jnp.int32)
    shard, row = wanted // ENTRIES, wanted % ENTRIES
    bias = jnp.where(shard // NZ == y, 0.0, FAR).astype(jnp.float32)
    place = (((row // 2) * NZ + (z + NZ - shard % NZ) % NZ) * BLOCK).astype(jnp.int32)
    lane = ((row % 2) * NLEN).astype(jnp.int32)
    messages = [None] * NY
    for k in (2, 1, 3, 0):
        out = attend(place[k], lane[k], bias[k], asked[k], table)
        messages[k] = shift(out, "y", -k) if k else out
    heads_out = combine(lambda_head, messages)

    heads = lax.all_to_all(
        heads_out.reshape(NX * NC, SPAN, WIDE), ("x", "c"), split_axis=0, concat_axis=0, tiled=True
    )
    rows = jnp.swapaxes(heads, 0, 1).reshape(SPAN, NX * NC * WIDE)
    return jnp.dot(rows, weight, preferred_element_type=jnp.float32).astype(jnp.bfloat16)


def solution(mesh):
    fine = Mesh(mesh.devices.reshape(NY, NZ, NX, NC), ("y", "z", "x", "c"))
    db, tp = ("y", "z"), ("x", "c")
    return jax.shard_map(
        on_device,
        mesh=fine,
        in_specs=(
            P(db, tp),
            P(db, None),
            P(db, None),
            P(db, None, tp),
            P(None, tp),
            P(None, tp),
            P(tp),
            P(tp, None),
        ),
        out_specs=P(db + tp, None),
        check_vma=False,
    )
```

```python
import functools
import jax
import jax.numpy as jnp
from jax import lax
from jax.experimental import pallas as pl
from jax.experimental.pallas import tpu as pltpu
from jax.sharding import Mesh, PartitionSpec as P

HD = 128
SPAN = 64
NLEN = 128
EPSILON = 1e-05
FAR = -1e30
NY, NZ, NX, NC = 4, 8, 4, 2
SPANS_DEV = 8
ENTRIES = 4
PAIRS = ENTRIES // 2
BLOCK = 4 * NLEN
QROWS = SPANS_DEV * SPAN
WIDE = 2 * HD
OROWS = SPANS_DEV * WIDE
VMEM_LIMIT = 48 * 1024 * 1024


def shift(a, axis, k):
    n = lax.axis_size(axis)
    return lax.ppermute(a, axis, [(i, (i + k) % n) for i in range(n)])


def ring_pieces(a, axis):
    n = lax.axis_size(axis)
    half = a.shape[0] // 2
    out = [(0, 0, a)]
    up = down = a
    for k in range(1, (n - 1) // 2 + 1):
        up, down = shift(up, axis, 1), shift(down, axis, -1)
        out += [(k, 0, up), (n - k, 0, down)]
    out += [(n // 2, 0, shift(up[:half], axis, 1)), (n // 2, half, shift(down[half:], axis, -1))]
    return out


def add_block(sums, tokens, key_rows, value_rows):
    f = tokens.astype(jnp.float32)
    terms = (
        jnp.dot(tokens, key_rows, preferred_element_type=jnp.float32),
        jnp.dot(tokens, value_rows, preferred_element_type=jnp.float32),
        jnp.sum(f * f, axis=1, keepdims=True),
    )
    return terms if sums is None else tuple(a + b for a, b in zip(sums, terms))


def weight_copies(feature_ref, key_ref, value_ref, places, sems):
    copies = []
    for i, (key_place, value_place) in enumerate(places):
        width = key_place.shape[0]
        at = pl.ds(pl.multiple_of(feature_ref[i] * width, width), width)
        copies.append(
            [
                pltpu.make_async_copy(key_ref.at[at], key_place, sems.at[2 * i]),
                pltpu.make_async_copy(value_ref.at[at], value_place, sems.at[2 * i + 1]),
            ]
        )
    for group in copies:
        for copy in group:
            copy.start()
    return copies


def early_kernel(feature_ref, *refs):
    pieces, rest = refs[:-7], refs[-7:]
    key_ref, value_ref, sum_ref, square_ref, late_ref, weights, sems = rest
    places = [(weights.at[2 * i], weights.at[2 * i + 1]) for i in range(len(pieces))]
    places += [(late_ref.at[2 * i], late_ref.at[2 * i + 1]) for i in range(late_ref.shape[0] // 2)]
    copies = weight_copies(feature_ref, key_ref, value_ref, places, sems)
    sums = None
    for i, piece in enumerate(pieces):
        for copy in copies[i]:
            copy.wait()
        sums = add_block(sums, piece[...], weights[2 * i], weights[2 * i + 1])
    sum_ref[:, :WIDE] = sums[0]
    sum_ref[:, WIDE:] = sums[1]
    square_ref[...] = jnp.broadcast_to(sums[2], square_ref.shape)
    for group in copies[len(pieces) :]:
        for copy in group:
            copy.wait()


def late_kernel(depth, *refs):
    *pieces, sum_ref, square_ref, weights, out_0, out_1 = refs
    for pair, out_ref in enumerate((out_0, out_1)):
        rows = slice(pair * 2 * NLEN, (pair + 1) * 2 * NLEN)
        sums = (sum_ref[rows, :WIDE], sum_ref[rows, WIDE:], square_ref[rows, :1])
        for i in range(len(pieces) // PAIRS):
            sums = add_block(
                sums, pieces[i * PAIRS + pair][...], weights[2 * i], weights[2 * i + 1]
            )
        inverse = lax.rsqrt(sums[2] / depth + EPSILON)
        out_ref[: 2 * NLEN, :] = (sums[0] * inverse).astype(jnp.bfloat16)
        out_ref[2 * NLEN :, :] = (sums[1] * inverse).T.astype(jnp.bfloat16)


def project_early(feature, pieces, key_weight, value_weight):
    tokens, width = pieces[0].shape
    blocks, count = feature.shape[0], len(pieces)
    vmem = pl.BlockSpec(memory_space=pltpu.VMEM)
    return pl.pallas_call(
        early_kernel,
        out_shape=[
            jax.ShapeDtypeStruct((tokens, 2 * WIDE), jnp.float32),
            jax.ShapeDtypeStruct((tokens, HD), jnp.float32),
            jax.ShapeDtypeStruct((2 * (blocks - count), width, WIDE), jnp.bfloat16),
        ],
        in_specs=[pl.BlockSpec(memory_space=pltpu.SMEM)]
        + [vmem] * count
        + [pl.BlockSpec(memory_space=pltpu.HBM)] * 2,
        out_specs=[vmem] * 3,
        scratch_shapes=[
            pltpu.VMEM((2 * count, width, WIDE), jnp.bfloat16),
            pltpu.SemaphoreType.DMA((2 * blocks,)),
        ],
        compiler_params=pltpu.CompilerParams(vmem_limit_bytes=VMEM_LIMIT),
        cost_estimate=pl.CostEstimate(
            flops=count * 512 * 512 * 1024, bytes_accessed=count << 20, transcendentals=0
        ),
        name="project_early",
    )(feature, *pieces, key_weight, value_weight)


def project_late(pieces, sums, depth):
    vmem = pl.BlockSpec(memory_space=pltpu.VMEM)
    return pl.pallas_call(
        functools.partial(late_kernel, depth),
        out_shape=[jax.ShapeDtypeStruct((BLOCK, WIDE), jnp.bfloat16)] * PAIRS,
        in_specs=[vmem] * (len(pieces) + len(sums)),
        out_specs=[vmem] * PAIRS,
        compiler_params=pltpu.CompilerParams(vmem_limit_bytes=VMEM_LIMIT),
        cost_estimate=pl.CostEstimate(
            flops=2 * 512 * 512 * 1024, bytes_accessed=2 << 20, transcendentals=0
        ),
        name="project_late",
    )(*pieces, *sums)


def attend_kernel(places, place_ref, lane_ref, bias_ref, query_ref, *refs):
    pieces = refs[: len(places)]
    out_ref, table, stats, sems = refs[len(places) :]
    copies = [
        pltpu.make_async_copy(piece, table.at[pl.ds(row, piece.shape[0])], sems.at[i])
        for i, (row, piece) in enumerate(zip(places, pieces))
    ]
    for copy in copies:
        copy.start()
    lane = lax.broadcasted_iota(jnp.int32, (SPAN, WIDE), 1)
    for copy in copies:
        copy.wait()
    group = 4
    for first in range(0, SPANS_DEV, group):
        scores, values = [], []
        for s in range(first, first + group):
            block = [pl.multiple_of(place_ref[2 * s + j], BLOCK) for j in range(2)]
            side = [pl.multiple_of(lane_ref[2 * s + j], NLEN) for j in range(2)]
            keys = [table[pl.ds(block[j] + side[j], NLEN), :] for j in range(2)]
            values.append(
                jnp.concatenate(
                    [
                        table[pl.ds(block[j] + 2 * NLEN, WIDE), pl.ds(side[j], NLEN)]
                        for j in range(2)
                    ],
                    axis=1,
                )
            )
            q = query_ref[s * SPAN : (s + 1) * SPAN, :]
            zero = jnp.zeros_like(q)
            both = jnp.concatenate(
                [jnp.where(lane < HD, q, zero), jnp.where(lane >= HD, q, zero)], axis=0
            )
            products = lax.dot_general(
                jnp.concatenate(keys, axis=0),
                both,
                (((1,), (1,)), ((), ())),
                preferred_element_type=jnp.float32,
            ) * (1.0 / HD**0.5)
            scores.append([products[j * NLEN : (j + 1) * NLEN] + bias_ref[2 * s + j] for j in range(2)])
        shares, levels = [], []
        for one, two in scores:
            top = jnp.max(jnp.maximum(one, two), axis=0, keepdims=True)
            one, two = jnp.exp(one - top), jnp.exp(two - top)
            total = jnp.sum(one + two, axis=0, keepdims=True)
            levels.append(top + jnp.log(total))
            inverse = 1.0 / total
            shares.append(
                jnp.concatenate([one * inverse, two * inverse], axis=0).astype(jnp.bfloat16)
            )
        attended = [
            jnp.dot(v, p, preferred_element_type=jnp.float32).astype(jnp.bfloat16)
            for v, p in zip(values, shares)
        ]
        for i, s in enumerate(range(first, first + group)):
            out_ref[s * WIDE : (s + 1) * WIDE, :] = attended[i]
            stats[s : s + 1, :] = levels[i]
    level = stats[...]
    high = level.astype(jnp.bfloat16).astype(jnp.float32)
    rest = level - high
    mid = rest.astype(jnp.bfloat16).astype(jnp.float32)
    low = rest - mid
    coded = jnp.concatenate([high, mid, low, jnp.zeros_like(low)], axis=0)
    out_ref[OROWS:, :] = coded.astype(jnp.bfloat16)


def attend(place, lane, bias, queries, pieces):
    places = tuple(row for row, _ in pieces)
    smem = pl.BlockSpec(memory_space=pltpu.SMEM)
    vmem = pl.BlockSpec(memory_space=pltpu.VMEM)
    return pl.pallas_call(
        functools.partial(attend_kernel, places),
        out_shape=jax.ShapeDtypeStruct((OROWS + 4 * SPANS_DEV, 2 * SPAN), jnp.bfloat16),
        in_specs=[smem] * 3 + [vmem] + [pl.BlockSpec(memory_space=pltpu.HBM)] * len(pieces),
        out_specs=vmem,
        scratch_shapes=[
            pltpu.VMEM((PAIRS * NZ * BLOCK, WIDE), jnp.bfloat16),
            pltpu.VMEM((SPANS_DEV, 2 * SPAN), jnp.float32),
            pltpu.SemaphoreType.DMA((len(pieces),)),
        ],
        compiler_params=pltpu.CompilerParams(vmem_limit_bytes=VMEM_LIMIT),
        cost_estimate=pl.CostEstimate(
            flops=1 << 29, bytes_accessed=6 << 20, transcendentals=1 << 18
        ),
        name="attend",
    )(place, lane, bias, queries, *[a for _, a in pieces])


def combine_kernel(side_ref, lambda_ref, *refs):
    *messages, mine_ref, theirs_ref = refs
    even = side_ref[0] == 0
    levels = []
    for message in messages:
        coded = message[OROWS:, :].astype(jnp.float32)
        n = SPANS_DEV
        levels.append((coded[:n] + coded[n : 2 * n]) + coded[2 * n : 3 * n])
    top = functools.reduce(jnp.maximum, levels)
    parts = [jnp.exp(level - top) for level in levels]
    total = functools.reduce(jnp.add, parts)
    lane = lax.broadcasted_iota(jnp.int32, (SPANS_DEV, 2 * SPAN), 1)
    sign = jnp.where(lane < SPAN, 1.0, -lambda_ref[0])
    factors = [part * (sign / total) for part in parts]
    first = lax.broadcasted_iota(jnp.int32, (WIDE, 2 * SPAN), 1) < SPAN
    for pair in range(SPANS_DEV // 2):
        both = []
        for s in (2 * pair, 2 * pair + 1):
            maps = functools.reduce(
                jnp.add,
                [
                    message[s * WIDE : (s + 1) * WIDE, :].astype(jnp.float32) * factor[s : s + 1, :]
                    for factor, message in zip(factors, messages)
                ],
            )
            both.append(maps + pltpu.roll(maps, SPAN, 1))
        attended = jnp.where(first, both[0], both[1])
        inverse = lax.rsqrt(jnp.mean(attended * attended, axis=0, keepdims=True) + EPSILON)
        rows = (attended * inverse).T.astype(jnp.bfloat16)
        mine_ref[pair] = jnp.where(even, rows[:SPAN], rows[SPAN:])
        theirs_ref[pair] = jnp.where(even, rows[SPAN:], rows[:SPAN])


def combine(side, lambda_head, messages):
    vmem = pl.BlockSpec(memory_space=pltpu.VMEM)
    return pl.pallas_call(
        combine_kernel,
        out_shape=[jax.ShapeDtypeStruct((SPANS_DEV // NC, SPAN, WIDE), jnp.bfloat16)] * NC,
        in_specs=[pl.BlockSpec(memory_space=pltpu.SMEM)] * 2 + [vmem] * NY,
        out_specs=[vmem] * NC,
        compiler_params=pltpu.CompilerParams(vmem_limit_bytes=VMEM_LIMIT),
        cost_estimate=pl.CostEstimate(
            flops=1 << 23, bytes_accessed=3 << 20, transcendentals=1 << 13
        ),
        name="combine",
    )(side, lambda_head, *messages)


def on_device(
    queries, nbr_shard, nbr_row, database, key_weight, value_weight, lambda_head, out_weight
):
    y, z = lax.axis_index("y"), lax.axis_index("z")
    x, c = lax.axis_index("x"), lax.axis_index("c")

    def feature(*offsets):
        return jnp.stack(
            [((x + NX - k) % NX) * NC + side for k in offsets for side in (c, 1 - c)]
        ).astype(jnp.int32)

    entry = (nbr_shard * ENTRIES + nbr_row).astype(jnp.bfloat16).reshape(1, -1)
    entry = jnp.pad(entry, ((0, 15), (0, WIDE - entry.shape[1])))
    packed = jnp.concatenate([queries, entry], axis=0)

    tokens = database.reshape(ENTRIES * NLEN, -1)
    half = tokens.shape[0] // 2
    up, down = shift(tokens, "x", 1), shift(tokens, "x", -1)
    above, below = shift(packed, "y", 1), shift(packed, "y", -1)
    above, below, packed, up, down = lax.optimization_barrier((above, below, packed, up, down))
    low, high = shift(up[:half], "x", 1), shift(down[half:], "x", -1)
    asked = [packed, above, shift(packed, "y", 2), below]
    early = [p for a in (tokens, up, down) for p in (a, shift(a, "c", 1))]
    sums = project_early(feature(0, 1, 3, 2), early, key_weight, value_weight)
    low, high, *sums = lax.optimization_barrier((low, high, *sums))
    late = [low, high, shift(low, "c", 1), shift(high, "c", 1)]
    asked[2], *late = lax.optimization_barrier((asked[2], *late))
    rows = project_late(late, sums, key_weight.shape[0])
    table = [
        ((pair * NZ + k) * BLOCK + r, a)
        for pair in range(PAIRS)
        for k, r, a in ring_pieces(rows[pair], "z")
    ]

    wanted = jnp.stack([a[QROWS, : 2 * SPANS_DEV] for a in asked]).astype(jnp.int32)
    shard, row = wanted // ENTRIES, wanted % ENTRIES
    bias = jnp.where(shard // NZ == y, 0.0, FAR).astype(jnp.float32)
    place = (((row // 2) * NZ + (z + NZ - shard % NZ) % NZ) * BLOCK).astype(jnp.int32)
    lane = ((row % 2) * NLEN).astype(jnp.int32)
    messages = [None] * NY
    for k in (2, 1, 3, 0):
        out = attend(place[k], lane[k], bias[k], asked[k], table)
        messages[k] = shift(out, "y", -k) if k else out
    weight = jnp.concatenate([out_weight, shift(out_weight, "c", 1)], axis=0)
    messages[0], weight = lax.optimization_barrier((messages[0], weight))
    mine, theirs = combine(c.astype(jnp.int32).reshape(1), lambda_head, messages)

    pair = jnp.concatenate([mine, shift(theirs, "c", 1)], axis=-1)

    def term(pair, k):
        rows = lax.dynamic_index_in_dim(pair, (x + k) % NX, axis=0, keepdims=False)
        return lax.optimization_barrier(jnp.dot(rows, weight, preferred_element_type=jnp.float32))

    def add(a, b):
        return (a.astype(jnp.float32) + b).astype(jnp.bfloat16)

    part = SPAN // 2
    far = term(pair, 2).astype(jnp.bfloat16)
    far, pair = lax.optimization_barrier((far, pair))
    up, down = shift(far[:part], "x", 1), shift(far[part:], "x", -1)
    near = term(pair, 1)
    up = jnp.concatenate([add(up, near[:part]), near[part:].astype(jnp.bfloat16)], axis=0)
    near = term(pair, 3)
    down = jnp.concatenate([near[:part].astype(jnp.bfloat16), add(down, near[part:])], axis=0)
    up, down = shift(up, "x", 1), shift(down, "x", -1)
    return (term(pair, 0) + up.astype(jnp.float32) + down.astype(jnp.float32)).astype(jnp.bfloat16)


def solution(mesh):
    fine = Mesh(mesh.devices.reshape(NY, NZ, NX, NC), ("y", "z", "x", "c"))
    db, tp = ("y", "z"), ("x", "c")
    return jax.shard_map(
        on_device,
        mesh=fine,
        in_specs=(
            P(db, tp),
            P(db, None),
            P(db, None),
            P(db, None, tp),
            P(None, tp),
            P(None, tp),
            P(tp),
            P(tp, None),
        ),
        out_specs=P(db + tp, None),
        check_vma=False,
    )
```

```python
import functools
import jax
import jax.numpy as jnp
from jax import lax
from jax.experimental import pallas as pl
from jax.experimental.pallas import tpu as pltpu
from jax.sharding import Mesh, PartitionSpec as P

HD = 128
SPAN = 64
NLEN = 128
EPSILON = 1e-05
FAR = -1e30
NY, NZ, NX, NC = 4, 8, 4, 2
SPANS_DEV = 8
ENTRIES = 4
PAIRS = ENTRIES // 2
BLOCK = 4 * NLEN
QROWS = SPANS_DEV * SPAN
WIDE = 2 * HD
OROWS = SPANS_DEV * WIDE
VMEM_LIMIT = 48 * 1024 * 1024


def shift(a, axis, k):
    n = lax.axis_size(axis)
    return lax.ppermute(a, axis, [(i, (i + k) % n) for i in range(n)])


def ring_pieces(a, axis):
    n = lax.axis_size(axis)
    half = a.shape[0] // 2
    out = [(0, 0, a)]
    up = down = a
    for k in range(1, (n - 1) // 2 + 1):
        up, down = shift(up, axis, 1), shift(down, axis, -1)
        out += [(k, 0, up), (n - k, 0, down)]
    out += [(n // 2, 0, shift(up[:half], axis, 1)), (n // 2, half, shift(down[half:], axis, -1))]
    return out


def add_block(sums, tokens, key_rows, value_rows):
    f = tokens.astype(jnp.float32)
    terms = (
        jnp.dot(tokens, key_rows, preferred_element_type=jnp.float32),
        jnp.dot(tokens, value_rows, preferred_element_type=jnp.float32),
        jnp.sum(f * f, axis=1, keepdims=True),
    )
    return terms if sums is None else tuple(a + b for a, b in zip(sums, terms))


def weight_copies(feature_ref, key_ref, value_ref, places, sems):
    copies = []
    for i, (key_place, value_place) in enumerate(places):
        width = key_place.shape[0]
        at = pl.ds(pl.multiple_of(feature_ref[i] * width, width), width)
        copies.append(
            [
                pltpu.make_async_copy(key_ref.at[at], key_place, sems.at[2 * i]),
                pltpu.make_async_copy(value_ref.at[at], value_place, sems.at[2 * i + 1]),
            ]
        )
    for group in copies:
        for copy in group:
            copy.start()
    return copies


def early_kernel(feature_ref, *refs):
    pieces, rest = refs[:-7], refs[-7:]
    key_ref, value_ref, sum_ref, square_ref, late_ref, weights, sems = rest
    places = [(weights.at[2 * i], weights.at[2 * i + 1]) for i in range(len(pieces))]
    places += [(late_ref.at[2 * i], late_ref.at[2 * i + 1]) for i in range(late_ref.shape[0] // 2)]
    copies = weight_copies(feature_ref, key_ref, value_ref, places, sems)
    sums = None
    for i, piece in enumerate(pieces):
        for copy in copies[i]:
            copy.wait()
        sums = add_block(sums, piece[...], weights[2 * i], weights[2 * i + 1])
    sum_ref[:, :WIDE] = sums[0]
    sum_ref[:, WIDE:] = sums[1]
    square_ref[...] = jnp.broadcast_to(sums[2], square_ref.shape)
    for group in copies[len(pieces) :]:
        for copy in group:
            copy.wait()


def late_kernel(depth, *refs):
    *pieces, sum_ref, square_ref, weights, out_0, out_1 = refs
    for pair, out_ref in enumerate((out_0, out_1)):
        rows = slice(pair * 2 * NLEN, (pair + 1) * 2 * NLEN)
        sums = (sum_ref[rows, :WIDE], sum_ref[rows, WIDE:], square_ref[rows, :1])
        for i in range(len(pieces) // PAIRS):
            sums = add_block(
                sums, pieces[i * PAIRS + pair][...], weights[2 * i], weights[2 * i + 1]
            )
        inverse = lax.rsqrt(sums[2] / depth + EPSILON)
        out_ref[: 2 * NLEN, :] = (sums[0] * inverse).astype(jnp.bfloat16)
        out_ref[2 * NLEN :, :] = (sums[1] * inverse).T.astype(jnp.bfloat16)


def project_early(feature, pieces, key_weight, value_weight):
    tokens, width = pieces[0].shape
    blocks, count = feature.shape[0], len(pieces)
    vmem = pl.BlockSpec(memory_space=pltpu.VMEM)
    return pl.pallas_call(
        early_kernel,
        out_shape=[
            jax.ShapeDtypeStruct((tokens, 2 * WIDE), jnp.float32),
            jax.ShapeDtypeStruct((tokens, HD), jnp.float32),
            jax.ShapeDtypeStruct((2 * (blocks - count), width, WIDE), jnp.bfloat16),
        ],
        in_specs=[pl.BlockSpec(memory_space=pltpu.SMEM)]
        + [vmem] * count
        + [pl.BlockSpec(memory_space=pltpu.HBM)] * 2,
        out_specs=[vmem] * 3,
        scratch_shapes=[
            pltpu.VMEM((2 * count, width, WIDE), jnp.bfloat16),
            pltpu.SemaphoreType.DMA((2 * blocks,)),
        ],
        compiler_params=pltpu.CompilerParams(vmem_limit_bytes=VMEM_LIMIT),
        cost_estimate=pl.CostEstimate(
            flops=count * 512 * 512 * 1024, bytes_accessed=count << 20, transcendentals=0
        ),
        name="project_early",
    )(feature, *pieces, key_weight, value_weight)


def project_late(pieces, sums, depth):
    vmem = pl.BlockSpec(memory_space=pltpu.VMEM)
    return pl.pallas_call(
        functools.partial(late_kernel, depth),
        out_shape=[jax.ShapeDtypeStruct((BLOCK, WIDE), jnp.bfloat16)] * PAIRS,
        in_specs=[vmem] * (len(pieces) + len(sums)),
        out_specs=[vmem] * PAIRS,
        compiler_params=pltpu.CompilerParams(vmem_limit_bytes=VMEM_LIMIT),
        cost_estimate=pl.CostEstimate(
            flops=2 * 512 * 512 * 1024, bytes_accessed=2 << 20, transcendentals=0
        ),
        name="project_late",
    )(*pieces, *sums)


def attend_kernel(places, place_ref, lane_ref, bias_ref, query_ref, *refs):
    pieces = refs[: len(places)]
    out_ref, table, stats, sems = refs[len(places) :]
    copies = [
        pltpu.make_async_copy(piece, table.at[pl.ds(row, piece.shape[0])], sems.at[i])
        for i, (row, piece) in enumerate(zip(places, pieces))
    ]
    for copy in copies:
        copy.start()
    lane = lax.broadcasted_iota(jnp.int32, (SPAN, WIDE), 1)
    for copy in copies:
        copy.wait()
    group = 4
    for first in range(0, SPANS_DEV, group):
        scores, values = [], []
        for s in range(first, first + group):
            block = [pl.multiple_of(place_ref[2 * s + j], BLOCK) for j in range(2)]
            side = [pl.multiple_of(lane_ref[2 * s + j], NLEN) for j in range(2)]
            keys = [table[pl.ds(block[j] + side[j], NLEN), :] for j in range(2)]
            values.append(
                jnp.concatenate(
                    [
                        table[pl.ds(block[j] + 2 * NLEN, WIDE), pl.ds(side[j], NLEN)]
                        for j in range(2)
                    ],
                    axis=1,
                )
            )
            q = query_ref[s * SPAN : (s + 1) * SPAN, :]
            zero = jnp.zeros_like(q)
            both = jnp.concatenate(
                [jnp.where(lane < HD, q, zero), jnp.where(lane >= HD, q, zero)], axis=0
            )
            products = lax.dot_general(
                jnp.concatenate(keys, axis=0),
                both,
                (((1,), (1,)), ((), ())),
                preferred_element_type=jnp.float32,
            ) * (1.0 / HD**0.5)
            scores.append([products[j * NLEN : (j + 1) * NLEN] + bias_ref[2 * s + j] for j in range(2)])
        shares, levels = [], []
        for one, two in scores:
            top = jnp.max(jnp.maximum(one, two), axis=0, keepdims=True)
            one, two = jnp.exp(one - top), jnp.exp(two - top)
            total = jnp.sum(one + two, axis=0, keepdims=True)
            levels.append(top + jnp.log(total))
            inverse = 1.0 / total
            shares.append(
                jnp.concatenate([one * inverse, two * inverse], axis=0).astype(jnp.bfloat16)
            )
        attended = [
            jnp.dot(v, p, preferred_element_type=jnp.float32).astype(jnp.bfloat16)
            for v, p in zip(values, shares)
        ]
        for i, s in enumerate(range(first, first + group)):
            out_ref[s * WIDE : (s + 1) * WIDE, :] = attended[i]
            stats[s : s + 1, :] = levels[i]
    level = stats[...]
    high = level.astype(jnp.bfloat16).astype(jnp.float32)
    rest = level - high
    mid = rest.astype(jnp.bfloat16).astype(jnp.float32)
    low = rest - mid
    coded = jnp.concatenate([high, mid, low, jnp.zeros_like(low)], axis=0)
    out_ref[OROWS:, :] = coded.astype(jnp.bfloat16)


def attend(place, lane, bias, queries, pieces):
    places = tuple(row for row, _ in pieces)
    smem = pl.BlockSpec(memory_space=pltpu.SMEM)
    vmem = pl.BlockSpec(memory_space=pltpu.VMEM)
    return pl.pallas_call(
        functools.partial(attend_kernel, places),
        out_shape=jax.ShapeDtypeStruct((OROWS + 4 * SPANS_DEV, 2 * SPAN), jnp.bfloat16),
        in_specs=[smem] * 3 + [vmem] + [pl.BlockSpec(memory_space=pltpu.HBM)] * len(pieces),
        out_specs=vmem,
        scratch_shapes=[
            pltpu.VMEM((PAIRS * NZ * BLOCK, WIDE), jnp.bfloat16),
            pltpu.VMEM((SPANS_DEV, 2 * SPAN), jnp.float32),
            pltpu.SemaphoreType.DMA((len(pieces),)),
        ],
        compiler_params=pltpu.CompilerParams(vmem_limit_bytes=VMEM_LIMIT),
        cost_estimate=pl.CostEstimate(
            flops=1 << 29, bytes_accessed=6 << 20, transcendentals=1 << 18
        ),
        name="attend",
    )(place, lane, bias, queries, *[a for _, a in pieces])


def combine_kernel(lambda_ref, *refs):
    *messages, out_ref = refs
    levels = []
    for message in messages:
        coded = message[OROWS:, :].astype(jnp.float32)
        n = SPANS_DEV
        levels.append((coded[:n] + coded[n : 2 * n]) + coded[2 * n : 3 * n])
    top = functools.reduce(jnp.maximum, levels)
    parts = [jnp.exp(level - top) for level in levels]
    total = functools.reduce(jnp.add, parts)
    lane = lax.broadcasted_iota(jnp.int32, (SPANS_DEV, 2 * SPAN), 1)
    sign = jnp.where(lane < SPAN, 1.0, -lambda_ref[0])
    factors = [part * (sign / total) for part in parts]
    first = lax.broadcasted_iota(jnp.int32, (WIDE, 2 * SPAN), 1) < SPAN
    for pair in range(SPANS_DEV // 2):
        both = []
        for s in (2 * pair, 2 * pair + 1):
            maps = functools.reduce(
                jnp.add,
                [
                    message[s * WIDE : (s + 1) * WIDE, :].astype(jnp.float32) * factor[s : s + 1, :]
                    for factor, message in zip(factors, messages)
                ],
            )
            both.append(maps + pltpu.roll(maps, SPAN, 1))
        attended = jnp.where(first, both[0], both[1])
        inverse = lax.rsqrt(jnp.mean(attended * attended, axis=0, keepdims=True) + EPSILON)
        out_ref[2 * pair * SPAN : 2 * (pair + 1) * SPAN, :] = (attended * inverse).T.astype(
            jnp.bfloat16
        )


def combine(lambda_head, messages):
    vmem = pl.BlockSpec(memory_space=pltpu.VMEM)
    return pl.pallas_call(
        combine_kernel,
        out_shape=jax.ShapeDtypeStruct((QROWS, WIDE), jnp.bfloat16),
        in_specs=[pl.BlockSpec(memory_space=pltpu.SMEM)] + [vmem] * NY,
        out_specs=vmem,
        compiler_params=pltpu.CompilerParams(vmem_limit_bytes=VMEM_LIMIT),
        cost_estimate=pl.CostEstimate(
            flops=1 << 23, bytes_accessed=3 << 20, transcendentals=1 << 13
        ),
        name="combine",
    )(lambda_head, *messages)


def on_device(
    queries, nbr_shard, nbr_row, database, key_weight, value_weight, lambda_head, out_weight
):
    y, z = lax.axis_index("y"), lax.axis_index("z")
    x, c = lax.axis_index("x"), lax.axis_index("c")

    def feature(*offsets):
        return jnp.stack(
            [((x + NX - k) % NX) * NC + side for k in offsets for side in (c, 1 - c)]
        ).astype(jnp.int32)

    entry = (nbr_shard * ENTRIES + nbr_row).astype(jnp.bfloat16).reshape(1, -1)
    entry = jnp.pad(entry, ((0, 15), (0, WIDE - entry.shape[1])))
    packed = jnp.concatenate([queries, entry], axis=0)

    tokens = database.reshape(ENTRIES * NLEN, -1)
    half = tokens.shape[0] // 2
    up, down = shift(tokens, "x", 1), shift(tokens, "x", -1)
    above, below = shift(packed, "y", 1), shift(packed, "y", -1)
    above, below, packed, up, down = lax.optimization_barrier((above, below, packed, up, down))
    low, high = shift(up[:half], "x", 1), shift(down[half:], "x", -1)
    early = [p for a in (tokens, up, down) for p in (a, shift(a, "c", 1))]
    sums = project_early(feature(0, 1, 3, 2), early, key_weight, value_weight)
    low, high, *sums = lax.optimization_barrier((low, high, *sums))
    late = [low, high, shift(low, "c", 1), shift(high, "c", 1)]
    rows = project_late(late, sums, key_weight.shape[0])
    table = [
        ((pair * NZ + k) * BLOCK + r, a)
        for pair in range(PAIRS)
        for k, r, a in ring_pieces(rows[pair], "z")
    ]

    after, _ = lax.optimization_barrier((packed, table[3][1]))
    asked = [packed, above, shift(after, "y", 2), below]

    held_back, _ = lax.optimization_barrier((out_weight, rows[0]))
    weight = lax.all_gather(held_back, ("x", "c"), axis=0, tiled=True)

    wanted = jnp.stack([a[QROWS, : 2 * SPANS_DEV] for a in asked]).astype(jnp.int32)
    shard, row = wanted // ENTRIES, wanted % ENTRIES
    bias = jnp.where(shard // NZ == y, 0.0, FAR).astype(jnp.float32)
    place = (((row // 2) * NZ + (z + NZ - shard % NZ) % NZ) * BLOCK).astype(jnp.int32)
    lane = ((row % 2) * NLEN).astype(jnp.int32)
    messages = [None] * NY
    for k in (2, 1, 3, 0):
        out = attend(place[k], lane[k], bias[k], asked[k], table)
        messages[k] = shift(out, "y", -k) if k else out
    heads_out = combine(lambda_head, messages)

    heads = lax.all_to_all(
        heads_out.reshape(NX * NC, SPAN, WIDE), ("x", "c"), split_axis=0, concat_axis=0, tiled=True
    )
    rows = jnp.swapaxes(heads, 0, 1).reshape(SPAN, NX * NC * WIDE)
    return jnp.dot(rows, weight, preferred_element_type=jnp.float32).astype(jnp.bfloat16)


def solution(mesh):
    fine = Mesh(mesh.devices.reshape(NY, NZ, NX, NC), ("y", "z", "x", "c"))
    db, tp = ("y", "z"), ("x", "c")
    return jax.shard_map(
        on_device,
        mesh=fine,
        in_specs=(
            P(db, tp),
            P(db, None),
            P(db, None),
            P(db, None, tp),
            P(None, tp),
            P(None, tp),
            P(tp),
            P(tp, None),
        ),
        out_specs=P(db + tp, None),
        check_vma=False,
    )
```

```python
import functools
import jax
import jax.numpy as jnp
from jax import lax
from jax.experimental import pallas as pl
from jax.experimental.pallas import tpu as pltpu
from jax.sharding import Mesh, PartitionSpec as P

HD = 128
SPAN = 64
NLEN = 128
EPSILON = 1e-05
FAR = -1e30
NY, NZ, NX, NC = 4, 8, 4, 2
SPANS_DEV = 8
ENTRIES = 4
PAIRS = ENTRIES // 2
BLOCK = 4 * NLEN
QROWS = SPANS_DEV * SPAN
WIDE = 2 * HD
OROWS = SPANS_DEV * WIDE
VMEM_LIMIT = 32 * 1024 * 1024
PROJECT_LIMIT = 48 * 1024 * 1024


def shift(a, axis, k):
    n = lax.axis_size(axis)
    return lax.ppermute(a, axis, [(i, (i + k) % n) for i in range(n)])


def ring_pieces(a, axis):
    n = lax.axis_size(axis)
    half = a.shape[0] // 2
    out = [(0, 0, a)]
    up = down = a
    for k in range(1, (n - 1) // 2 + 1):
        up, down = shift(up, axis, 1), shift(down, axis, -1)
        out += [(k, 0, up), (n - k, 0, down)]
    out += [(n // 2, 0, shift(up[:half], axis, 1)), (n // 2, half, shift(down[half:], axis, -1))]
    return out


def add_block(sums, tokens, key_rows, value_rows):
    f = tokens.astype(jnp.float32)
    terms = (
        jnp.dot(tokens, key_rows, preferred_element_type=jnp.float32),
        jnp.dot(tokens, value_rows, preferred_element_type=jnp.float32),
        jnp.sum(f * f, axis=1, keepdims=True),
    )
    return terms if sums is None else tuple(a + b for a, b in zip(sums, terms))


def weight_copies(feature_ref, key_ref, value_ref, places, sems):
    copies = []
    for i, (key_place, value_place) in enumerate(places):
        width = key_place.shape[0]
        at = pl.ds(pl.multiple_of(feature_ref[i] * width, width), width)
        copies.append(
            [
                pltpu.make_async_copy(key_ref.at[at], key_place, sems.at[2 * i]),
                pltpu.make_async_copy(value_ref.at[at], value_place, sems.at[2 * i + 1]),
            ]
        )
    for group in copies:
        for copy in group:
            copy.start()
    return copies


def early_kernel(feature_ref, *refs):
    pieces, rest = refs[:-7], refs[-7:]
    key_ref, value_ref, sum_ref, square_ref, late_ref, weights, sems = rest
    places = [(weights.at[2 * i], weights.at[2 * i + 1]) for i in range(len(pieces))]
    places += [(late_ref.at[2 * i], late_ref.at[2 * i + 1]) for i in range(late_ref.shape[0] // 2)]
    copies = weight_copies(feature_ref, key_ref, value_ref, places, sems)
    sums = None
    for i, piece in enumerate(pieces):
        for copy in copies[i]:
            copy.wait()
        sums = add_block(sums, piece[...], weights[2 * i], weights[2 * i + 1])
    sum_ref[:, :WIDE] = sums[0]
    sum_ref[:, WIDE:] = sums[1]
    square_ref[...] = jnp.broadcast_to(sums[2], square_ref.shape)
    for group in copies[len(pieces) :]:
        for copy in group:
            copy.wait()


def late_kernel(depth, *refs):
    *pieces, sum_ref, square_ref, weights, out_0, out_1 = refs
    for pair, out_ref in enumerate((out_0, out_1)):
        rows = slice(pair * 2 * NLEN, (pair + 1) * 2 * NLEN)
        sums = (sum_ref[rows, :WIDE], sum_ref[rows, WIDE:], square_ref[rows, :1])
        for i in range(len(pieces) // PAIRS):
            sums = add_block(
                sums, pieces[i * PAIRS + pair][...], weights[2 * i], weights[2 * i + 1]
            )
        inverse = lax.rsqrt(sums[2] / depth + EPSILON)
        out_ref[: 2 * NLEN, :] = (sums[0] * inverse).astype(jnp.bfloat16)
        out_ref[2 * NLEN :, :] = (sums[1] * inverse).T.astype(jnp.bfloat16)


def project_early(feature, pieces, key_weight, value_weight):
    tokens, width = pieces[0].shape
    blocks, count = feature.shape[0], len(pieces)
    vmem = pl.BlockSpec(memory_space=pltpu.VMEM)
    return pl.pallas_call(
        early_kernel,
        out_shape=[
            jax.ShapeDtypeStruct((tokens, 2 * WIDE), jnp.float32),
            jax.ShapeDtypeStruct((tokens, HD), jnp.float32),
            jax.ShapeDtypeStruct((2 * (blocks - count), width, WIDE), jnp.bfloat16),
        ],
        in_specs=[pl.BlockSpec(memory_space=pltpu.SMEM)]
        + [vmem] * count
        + [pl.BlockSpec(memory_space=pltpu.HBM)] * 2,
        out_specs=[vmem] * 3,
        scratch_shapes=[
            pltpu.VMEM((2 * count, width, WIDE), jnp.bfloat16),
            pltpu.SemaphoreType.DMA((2 * blocks,)),
        ],
        compiler_params=pltpu.CompilerParams(vmem_limit_bytes=PROJECT_LIMIT),
        cost_estimate=pl.CostEstimate(
            flops=count * 512 * 512 * 1024, bytes_accessed=count << 20, transcendentals=0
        ),
        name="project_early",
    )(feature, *pieces, key_weight, value_weight)


def project_late(pieces, sums, depth):
    vmem = pl.BlockSpec(memory_space=pltpu.VMEM)
    return pl.pallas_call(
        functools.partial(late_kernel, depth),
        out_shape=[jax.ShapeDtypeStruct((BLOCK, WIDE), jnp.bfloat16)] * PAIRS,
        in_specs=[vmem] * (len(pieces) + len(sums)),
        out_specs=[vmem] * PAIRS,
        compiler_params=pltpu.CompilerParams(vmem_limit_bytes=PROJECT_LIMIT),
        cost_estimate=pl.CostEstimate(
            flops=2 * 512 * 512 * 1024, bytes_accessed=2 << 20, transcendentals=0
        ),
        name="project_late",
    )(*pieces, *sums)


def gather_table(places, pieces, table, sems):
    copies = [
        pltpu.make_async_copy(piece, table.at[pl.ds(row, piece.shape[0])], sems.at[i])
        for i, (row, piece) in enumerate(zip(places, pieces))
    ]
    for copy in copies:
        copy.start()
    for copy in copies:
        copy.wait()


def first_kernel(places, place_ref, lane_ref, bias_ref, query_ref, *refs):
    pieces, (out_ref, table, stats, sems) = refs[: len(places)], refs[len(places) :]
    gather_table(places, pieces, table, sems)
    attend_kernel(place_ref, lane_ref, bias_ref, query_ref, table, out_ref, stats)


def attend_kernel(place_ref, lane_ref, bias_ref, query_ref, table, out_ref, stats):
    lane = lax.broadcasted_iota(jnp.int32, (SPAN, WIDE), 1)
    group = 4
    for first in range(0, SPANS_DEV, group):
        scores, values = [], []
        for s in range(first, first + group):
            block = [pl.multiple_of(place_ref[2 * s + j], BLOCK) for j in range(2)]
            side = [pl.multiple_of(lane_ref[2 * s + j], NLEN) for j in range(2)]
            keys = [table[pl.ds(block[j] + side[j], NLEN), :] for j in range(2)]
            values.append(
                jnp.concatenate(
                    [
                        table[pl.ds(block[j] + 2 * NLEN, WIDE), pl.ds(side[j], NLEN)]
                        for j in range(2)
                    ],
                    axis=1,
                )
            )
            q = query_ref[s * SPAN : (s + 1) * SPAN, :]
            zero = jnp.zeros_like(q)
            both = jnp.concatenate(
                [jnp.where(lane < HD, q, zero), jnp.where(lane >= HD, q, zero)], axis=0
            )
            products = lax.dot_general(
                jnp.concatenate(keys, axis=0),
                both,
                (((1,), (1,)), ((), ())),
                preferred_element_type=jnp.float32,
            ) * (1.0 / HD**0.5)
            scores.append([products[j * NLEN : (j + 1) * NLEN] + bias_ref[2 * s + j] for j in range(2)])
        shares, levels = [], []
        for one, two in scores:
            top = jnp.max(jnp.maximum(one, two), axis=0, keepdims=True)
            one, two = jnp.exp(one - top), jnp.exp(two - top)
            total = jnp.sum(one + two, axis=0, keepdims=True)
            levels.append(top + jnp.log(total))
            inverse = 1.0 / total
            shares.append(
                jnp.concatenate([one * inverse, two * inverse], axis=0).astype(jnp.bfloat16)
            )
        attended = [
            jnp.dot(v, p, preferred_element_type=jnp.float32).astype(jnp.bfloat16)
            for v, p in zip(values, shares)
        ]
        for i, s in enumerate(range(first, first + group)):
            out_ref[s * WIDE : (s + 1) * WIDE, :] = attended[i]
            stats[s : s + 1, :] = levels[i]
    level = stats[...]
    high = level.astype(jnp.bfloat16).astype(jnp.float32)
    rest = level - high
    mid = rest.astype(jnp.bfloat16).astype(jnp.float32)
    low = rest - mid
    coded = jnp.concatenate([high, mid, low, jnp.zeros_like(low)], axis=0)
    out_ref[OROWS:, :] = coded.astype(jnp.bfloat16)


def attend(place, lane, bias, queries, pieces, table=None):
    places = tuple(row for row, _ in pieces)
    smem = pl.BlockSpec(memory_space=pltpu.SMEM)
    vmem = pl.BlockSpec(memory_space=pltpu.VMEM)
    message = jax.ShapeDtypeStruct((OROWS + 4 * SPANS_DEV, 2 * SPAN), jnp.bfloat16)
    whole = jax.ShapeDtypeStruct((PAIRS * NZ * BLOCK, WIDE), jnp.bfloat16)
    stats = pltpu.VMEM((SPANS_DEV, 2 * SPAN), jnp.float32)
    cost = pl.CostEstimate(flops=1 << 29, bytes_accessed=6 << 20, transcendentals=1 << 18)
    params = pltpu.CompilerParams(vmem_limit_bytes=VMEM_LIMIT)
    if table is None:
        return pl.pallas_call(
            functools.partial(first_kernel, places),
            out_shape=[message, whole],
            in_specs=[smem] * 3 + [vmem] + [pl.BlockSpec(memory_space=pltpu.HBM)] * len(pieces),
            out_specs=[vmem, vmem],
            scratch_shapes=[stats, pltpu.SemaphoreType.DMA((len(pieces),))],
            compiler_params=params,
            cost_estimate=cost,
            name="attend_first",
        )(place, lane, bias, queries, *[a for _, a in pieces])
    out = pl.pallas_call(
        attend_kernel,
        out_shape=message,
        in_specs=[smem] * 3 + [vmem] * 2,
        out_specs=vmem,
        scratch_shapes=[stats],
        compiler_params=params,
        cost_estimate=cost,
        name="attend",
    )(place, lane, bias, queries, table)
    return out, table


def combine_kernel(lambda_ref, *refs):
    *messages, out_ref = refs
    levels = []
    for message in messages:
        coded = message[OROWS:, :].astype(jnp.float32)
        n = SPANS_DEV
        levels.append((coded[:n] + coded[n : 2 * n]) + coded[2 * n : 3 * n])
    top = functools.reduce(jnp.maximum, levels)
    parts = [jnp.exp(level - top) for level in levels]
    total = functools.reduce(jnp.add, parts)
    lane = lax.broadcasted_iota(jnp.int32, (SPANS_DEV, 2 * SPAN), 1)
    sign = jnp.where(lane < SPAN, 1.0, -lambda_ref[0])
    factors = [part * (sign / total) for part in parts]
    first = lax.broadcasted_iota(jnp.int32, (WIDE, 2 * SPAN), 1) < SPAN
    for pair in range(SPANS_DEV // 2):
        both = []
        for s in (2 * pair, 2 * pair + 1):
            maps = functools.reduce(
                jnp.add,
                [
                    message[s * WIDE : (s + 1) * WIDE, :].astype(jnp.float32) * factor[s : s + 1, :]
                    for factor, message in zip(factors, messages)
                ],
            )
            both.append(maps + pltpu.roll(maps, SPAN, 1))
        attended = jnp.where(first, both[0], both[1])
        inverse = lax.rsqrt(jnp.mean(attended * attended, axis=0, keepdims=True) + EPSILON)
        out_ref[2 * pair * SPAN : 2 * (pair + 1) * SPAN, :] = (attended * inverse).T.astype(
            jnp.bfloat16
        )


def combine(lambda_head, messages):
    vmem = pl.BlockSpec(memory_space=pltpu.VMEM)
    return pl.pallas_call(
        combine_kernel,
        out_shape=jax.ShapeDtypeStruct((QROWS, WIDE), jnp.bfloat16),
        in_specs=[pl.BlockSpec(memory_space=pltpu.SMEM)] + [vmem] * NY,
        out_specs=vmem,
        compiler_params=pltpu.CompilerParams(vmem_limit_bytes=VMEM_LIMIT),
        cost_estimate=pl.CostEstimate(
            flops=1 << 23, bytes_accessed=3 << 20, transcendentals=1 << 13
        ),
        name="combine",
    )(lambda_head, *messages)


def on_device(
    queries, nbr_shard, nbr_row, database, key_weight, value_weight, lambda_head, out_weight
):
    y, z = lax.axis_index("y"), lax.axis_index("z")
    x, c = lax.axis_index("x"), lax.axis_index("c")

    def feature(*offsets):
        return jnp.stack(
            [((x + NX - k) % NX) * NC + side for k in offsets for side in (c, 1 - c)]
        ).astype(jnp.int32)

    entry = (nbr_shard * ENTRIES + nbr_row).astype(jnp.bfloat16).reshape(1, -1)
    entry = jnp.pad(entry, ((0, 15), (0, WIDE - entry.shape[1])))
    packed = jnp.concatenate([queries, entry], axis=0)

    tokens = database.reshape(ENTRIES * NLEN, -1)
    half = tokens.shape[0] // 2
    up, down = shift(tokens, "x", 1), shift(tokens, "x", -1)
    above, below = shift(packed, "y", 1), shift(packed, "y", -1)
    above, below, packed, up, down = lax.optimization_barrier((above, below, packed, up, down))
    low, high = shift(up[:half], "x", 1), shift(down[half:], "x", -1)
    early = [p for a in (tokens, up, down) for p in (a, shift(a, "c", 1))]
    sums = project_early(feature(0, 1, 3, 2), early, key_weight, value_weight)
    low, high, *sums = lax.optimization_barrier((low, high, *sums))
    late = [low, high, shift(low, "c", 1), shift(high, "c", 1)]
    rows = project_late(late, sums, key_weight.shape[0])
    table = [
        ((pair * NZ + k) * BLOCK + r, a)
        for pair in range(PAIRS)
        for k, r, a in ring_pieces(rows[pair], "z")
    ]

    after, _ = lax.optimization_barrier((packed, table[3][1]))
    asked = [packed, above, shift(after, "y", 2), below]

    held_back, _ = lax.optimization_barrier((out_weight, rows[0]))
    weight = lax.all_gather(held_back, ("x", "c"), axis=0, tiled=True)

    wanted = jnp.stack([a[QROWS, : 2 * SPANS_DEV] for a in asked]).astype(jnp.int32)
    shard, row = wanted // ENTRIES, wanted % ENTRIES
    bias = jnp.where(shard // NZ == y, 0.0, FAR).astype(jnp.float32)
    place = (((row // 2) * NZ + (z + NZ - shard % NZ) % NZ) * BLOCK).astype(jnp.int32)
    lane = ((row % 2) * NLEN).astype(jnp.int32)
    messages, whole = [None] * NY, None
    for k in (2, 1, 3, 0):
        out, whole = attend(place[k], lane[k], bias[k], asked[k], table, whole)
        messages[k] = shift(out, "y", -k) if k else out
    heads_out = combine(lambda_head, messages)

    heads = lax.all_to_all(
        heads_out.reshape(NX * NC, SPAN, WIDE), ("x", "c"), split_axis=0, concat_axis=0, tiled=True
    )
    rows = jnp.swapaxes(heads, 0, 1).reshape(SPAN, NX * NC * WIDE)
    return jnp.dot(rows, weight, preferred_element_type=jnp.float32).astype(jnp.bfloat16)


def solution(mesh):
    fine = Mesh(mesh.devices.reshape(NY, NZ, NX, NC), ("y", "z", "x", "c"))
    db, tp = ("y", "z"), ("x", "c")
    return jax.shard_map(
        on_device,
        mesh=fine,
        in_specs=(
            P(db, tp),
            P(db, None),
            P(db, None),
            P(db, None, tp),
            P(None, tp),
            P(None, tp),
            P(tp),
            P(tp, None),
        ),
        out_specs=P(db + tp, None),
        check_vma=False,
    )
```

```python
import functools
import jax
import jax.numpy as jnp
from jax import lax
from jax.experimental import pallas as pl
from jax.experimental.pallas import tpu as pltpu
from jax.sharding import Mesh, PartitionSpec as P

HD = 128
SPAN = 64
NLEN = 128
EPSILON = 1e-05
FAR = -1e30
NY, NZ, NX, NC = 4, 8, 4, 2
SPANS_DEV = 8
ENTRIES = 4
PAIRS = ENTRIES // 2
BLOCK = 4 * NLEN
QROWS = SPANS_DEV * SPAN
WIDE = 2 * HD
OROWS = SPANS_DEV * WIDE
VMEM_LIMIT = 48 * 1024 * 1024


def shift(a, axis, k):
    n = lax.axis_size(axis)
    return lax.ppermute(a, axis, [(i, (i + k) % n) for i in range(n)])


def ring_pieces(a, axis):
    n = lax.axis_size(axis)
    half = a.shape[0] // 2
    out = [(0, 0, a)]
    up = down = a
    for k in range(1, (n - 1) // 2 + 1):
        up, down = shift(up, axis, 1), shift(down, axis, -1)
        out += [(k, 0, up), (n - k, 0, down)]
    out += [(n // 2, 0, shift(up[:half], axis, 1)), (n // 2, half, shift(down[half:], axis, -1))]
    return out


def add_block(sums, tokens, key_rows, value_rows):
    f = tokens.astype(jnp.float32)
    terms = (
        jnp.dot(tokens, key_rows, preferred_element_type=jnp.float32),
        jnp.dot(tokens, value_rows, preferred_element_type=jnp.float32),
        jnp.sum(f * f, axis=1, keepdims=True),
    )
    return terms if sums is None else tuple(a + b for a, b in zip(sums, terms))


def weight_copies(feature_ref, key_ref, value_ref, places, sems):
    copies = []
    for i, (key_place, value_place) in enumerate(places):
        width = key_place.shape[0]
        at = pl.ds(pl.multiple_of(feature_ref[i] * width, width), width)
        copies.append(
            [
                pltpu.make_async_copy(key_ref.at[at], key_place, sems.at[2 * i]),
                pltpu.make_async_copy(value_ref.at[at], value_place, sems.at[2 * i + 1]),
            ]
        )
    for group in copies:
        for copy in group:
            copy.start()
    return copies


def early_kernel(feature_ref, *refs):
    pieces, rest = refs[:-7], refs[-7:]
    key_ref, value_ref, sum_ref, square_ref, late_ref, weights, sems = rest
    places = [(weights.at[2 * i], weights.at[2 * i + 1]) for i in range(len(pieces))]
    places += [(late_ref.at[2 * i], late_ref.at[2 * i + 1]) for i in range(late_ref.shape[0] // 2)]
    copies = weight_copies(feature_ref, key_ref, value_ref, places, sems)
    sums = None
    for i, piece in enumerate(pieces):
        for copy in copies[i]:
            copy.wait()
        sums = add_block(sums, piece[...], weights[2 * i], weights[2 * i + 1])
    sum_ref[:, :WIDE] = sums[0]
    sum_ref[:, WIDE:] = sums[1]
    square_ref[...] = jnp.broadcast_to(sums[2], square_ref.shape)
    for group in copies[len(pieces) :]:
        for copy in group:
            copy.wait()


def late_kernel(depth, *refs):
    *pieces, sum_ref, square_ref, weights, out_0, out_1 = refs
    for pair, out_ref in enumerate((out_0, out_1)):
        rows = slice(pair * 2 * NLEN, (pair + 1) * 2 * NLEN)
        sums = (sum_ref[rows, :WIDE], sum_ref[rows, WIDE:], square_ref[rows, :1])
        for i in range(len(pieces) // PAIRS):
            sums = add_block(
                sums, pieces[i * PAIRS + pair][...], weights[2 * i], weights[2 * i + 1]
            )
        inverse = lax.rsqrt(sums[2] / depth + EPSILON)
        out_ref[: 2 * NLEN, :] = (sums[0] * inverse).astype(jnp.bfloat16)
        out_ref[2 * NLEN :, :] = (sums[1] * inverse).T.astype(jnp.bfloat16)


def project_early(feature, pieces, key_weight, value_weight):
    tokens, width = pieces[0].shape
    blocks, count = feature.shape[0], len(pieces)
    vmem = pl.BlockSpec(memory_space=pltpu.VMEM)
    return pl.pallas_call(
        early_kernel,
        out_shape=[
            jax.ShapeDtypeStruct((tokens, 2 * WIDE), jnp.float32),
            jax.ShapeDtypeStruct((tokens, HD), jnp.float32),
            jax.ShapeDtypeStruct((2 * (blocks - count), width, WIDE), jnp.bfloat16),
        ],
        in_specs=[pl.BlockSpec(memory_space=pltpu.SMEM)]
        + [vmem] * count
        + [pl.BlockSpec(memory_space=pltpu.HBM)] * 2,
        out_specs=[vmem] * 3,
        scratch_shapes=[
            pltpu.VMEM((2 * count, width, WIDE), jnp.bfloat16),
            pltpu.SemaphoreType.DMA((2 * blocks,)),
        ],
        compiler_params=pltpu.CompilerParams(vmem_limit_bytes=VMEM_LIMIT),
        cost_estimate=pl.CostEstimate(
            flops=count * 512 * 512 * 1024, bytes_accessed=count << 20, transcendentals=0
        ),
        name="project_early",
    )(feature, *pieces, key_weight, value_weight)


def project_late(pieces, sums, depth):
    vmem = pl.BlockSpec(memory_space=pltpu.VMEM)
    return pl.pallas_call(
        functools.partial(late_kernel, depth),
        out_shape=[jax.ShapeDtypeStruct((BLOCK, WIDE), jnp.bfloat16)] * PAIRS,
        in_specs=[vmem] * (len(pieces) + len(sums)),
        out_specs=[vmem] * PAIRS,
        compiler_params=pltpu.CompilerParams(vmem_limit_bytes=VMEM_LIMIT),
        cost_estimate=pl.CostEstimate(
            flops=2 * 512 * 512 * 1024, bytes_accessed=2 << 20, transcendentals=0
        ),
        name="project_late",
    )(*pieces, *sums)


def attend_kernel(places, place_ref, lane_ref, bias_ref, query_ref, *refs):
    pieces = refs[: len(places)]
    out_ref, table, stats, sems = refs[len(places) :]
    copies = [
        pltpu.make_async_copy(piece, table.at[pl.ds(row, piece.shape[0])], sems.at[i])
        for i, (row, piece) in enumerate(zip(places, pieces))
    ]
    for copy in copies:
        copy.start()
    lane = lax.broadcasted_iota(jnp.int32, (SPAN, WIDE), 1)
    for copy in copies:
        copy.wait()
    group = 4
    for first in range(0, SPANS_DEV, group):
        scores, values = [], []
        for s in range(first, first + group):
            block = [pl.multiple_of(place_ref[2 * s + j], BLOCK) for j in range(2)]
            side = [pl.multiple_of(lane_ref[2 * s + j], NLEN) for j in range(2)]
            keys = [table[pl.ds(block[j] + side[j], NLEN), :] for j in range(2)]
            values.append(
                jnp.concatenate(
                    [
                        table[pl.ds(block[j] + 2 * NLEN, WIDE), pl.ds(side[j], NLEN)]
                        for j in range(2)
                    ],
                    axis=1,
                )
            )
            q = query_ref[s * SPAN : (s + 1) * SPAN, :]
            zero = jnp.zeros_like(q)
            both = jnp.concatenate(
                [jnp.where(lane < HD, q, zero), jnp.where(lane >= HD, q, zero)], axis=0
            )
            products = lax.dot_general(
                jnp.concatenate(keys, axis=0),
                both,
                (((1,), (1,)), ((), ())),
                preferred_element_type=jnp.float32,
            ) * (1.0 / HD**0.5)
            scores.append([products[j * NLEN : (j + 1) * NLEN] + bias_ref[2 * s + j] for j in range(2)])
        shares, levels = [], []
        for one, two in scores:
            top = jnp.max(jnp.maximum(one, two), axis=0, keepdims=True)
            one, two = jnp.exp(one - top), jnp.exp(two - top)
            total = jnp.sum(one + two, axis=0, keepdims=True)
            levels.append(top + jnp.log(total))
            inverse = 1.0 / total
            shares.append(
                jnp.concatenate([one * inverse, two * inverse], axis=0).astype(jnp.bfloat16)
            )
        attended = [
            jnp.dot(v, p, preferred_element_type=jnp.float32).astype(jnp.bfloat16)
            for v, p in zip(values, shares)
        ]
        for i, s in enumerate(range(first, first + group)):
            out_ref[s * WIDE : (s + 1) * WIDE, :] = attended[i]
            stats[s : s + 1, :] = levels[i]
    level = stats[...]
    high = level.astype(jnp.bfloat16).astype(jnp.float32)
    rest = level - high
    mid = rest.astype(jnp.bfloat16).astype(jnp.float32)
    low = rest - mid
    coded = jnp.concatenate([high, mid, low, jnp.zeros_like(low)], axis=0)
    out_ref[OROWS:, :] = coded.astype(jnp.bfloat16)


def attend(place, lane, bias, queries, pieces):
    places = tuple(row for row, _ in pieces)
    smem = pl.BlockSpec(memory_space=pltpu.SMEM)
    vmem = pl.BlockSpec(memory_space=pltpu.VMEM)
    return pl.pallas_call(
        functools.partial(attend_kernel, places),
        out_shape=jax.ShapeDtypeStruct((OROWS + 4 * SPANS_DEV, 2 * SPAN), jnp.bfloat16),
        in_specs=[smem] * 3 + [vmem] + [pl.BlockSpec(memory_space=pltpu.HBM)] * len(pieces),
        out_specs=vmem,
        scratch_shapes=[
            pltpu.VMEM((PAIRS * NZ * BLOCK, WIDE), jnp.bfloat16),
            pltpu.VMEM((SPANS_DEV, 2 * SPAN), jnp.float32),
            pltpu.SemaphoreType.DMA((len(pieces),)),
        ],
        compiler_params=pltpu.CompilerParams(vmem_limit_bytes=VMEM_LIMIT),
        cost_estimate=pl.CostEstimate(
            flops=1 << 29, bytes_accessed=6 << 20, transcendentals=1 << 18
        ),
        name="attend",
    )(place, lane, bias, queries, *[a for _, a in pieces])


def combine_kernel(lambda_ref, *refs):
    *messages, out_ref = refs
    levels = []
    for message in messages:
        coded = message[OROWS:, :].astype(jnp.float32)
        n = SPANS_DEV
        levels.append((coded[:n] + coded[n : 2 * n]) + coded[2 * n : 3 * n])
    top = functools.reduce(jnp.maximum, levels)
    parts = [jnp.exp(level - top) for level in levels]
    total = functools.reduce(jnp.add, parts)
    lane = lax.broadcasted_iota(jnp.int32, (SPANS_DEV, 2 * SPAN), 1)
    sign = jnp.where(lane < SPAN, 1.0, -lambda_ref[0])
    factors = [part * (sign / total) for part in parts]
    first = lax.broadcasted_iota(jnp.int32, (WIDE, 2 * SPAN), 1) < SPAN
    for pair in range(SPANS_DEV // 2):
        both = []
        for s in (2 * pair, 2 * pair + 1):
            maps = functools.reduce(
                jnp.add,
                [
                    message[s * WIDE : (s + 1) * WIDE, :].astype(jnp.float32) * factor[s : s + 1, :]
                    for factor, message in zip(factors, messages)
                ],
            )
            both.append(maps + pltpu.roll(maps, SPAN, 1))
        attended = jnp.where(first, both[0], both[1])
        inverse = lax.rsqrt(jnp.mean(attended * attended, axis=0, keepdims=True) + EPSILON)
        out_ref[2 * pair * SPAN : 2 * (pair + 1) * SPAN, :] = (attended * inverse).T.astype(
            jnp.bfloat16
        )


def combine(lambda_head, messages):
    vmem = pl.BlockSpec(memory_space=pltpu.VMEM)
    return pl.pallas_call(
        combine_kernel,
        out_shape=jax.ShapeDtypeStruct((QROWS, WIDE), jnp.bfloat16),
        in_specs=[pl.BlockSpec(memory_space=pltpu.SMEM)] + [vmem] * NY,
        out_specs=vmem,
        compiler_params=pltpu.CompilerParams(vmem_limit_bytes=VMEM_LIMIT),
        cost_estimate=pl.CostEstimate(
            flops=1 << 23, bytes_accessed=3 << 20, transcendentals=1 << 13
        ),
        name="combine",
    )(lambda_head, *messages)


def output_kernel(heads_ref, weight_ref, out_ref, total):
    step = pl.program_id(0)
    term = jnp.dot(heads_ref[0], weight_ref[...], preferred_element_type=jnp.float32)

    @pl.when(step == 0)
    def _():
        total[...] = term

    @pl.when(step > 0)
    def _():
        total[...] += term

    @pl.when(step == pl.num_programs(0) - 1)
    def _():
        out_ref[...] = total[...].astype(jnp.bfloat16)


def output(heads, weight):
    count, rows, depth = heads.shape
    width = weight.shape[1]
    return pl.pallas_call(
        output_kernel,
        grid=(count,),
        out_shape=jax.ShapeDtypeStruct((rows, width), jnp.bfloat16),
        in_specs=[
            pl.BlockSpec((1, rows, depth), lambda i: (i, 0, 0)),
            pl.BlockSpec((depth, width), lambda i: (i, 0)),
        ],
        out_specs=pl.BlockSpec((rows, width), lambda i: (0, 0)),
        scratch_shapes=[pltpu.VMEM((rows, width), jnp.float32)],
        compiler_params=pltpu.CompilerParams(vmem_limit_bytes=VMEM_LIMIT),
        cost_estimate=pl.CostEstimate(
            flops=2 * 64 * 2048 * 4096, bytes_accessed=16 << 20, transcendentals=0
        ),
        name="output",
    )(heads, weight)


def on_device(
    queries, nbr_shard, nbr_row, database, key_weight, value_weight, lambda_head, out_weight
):
    y, z = lax.axis_index("y"), lax.axis_index("z")
    x, c = lax.axis_index("x"), lax.axis_index("c")

    def feature(*offsets):
        return jnp.stack(
            [((x + NX - k) % NX) * NC + side for k in offsets for side in (c, 1 - c)]
        ).astype(jnp.int32)

    entry = (nbr_shard * ENTRIES + nbr_row).astype(jnp.bfloat16).reshape(1, -1)
    entry = jnp.pad(entry, ((0, 15), (0, WIDE - entry.shape[1])))
    packed = jnp.concatenate([queries, entry], axis=0)

    tokens = database.reshape(ENTRIES * NLEN, -1)
    half = tokens.shape[0] // 2
    up, down = shift(tokens, "x", 1), shift(tokens, "x", -1)
    above, below = shift(packed, "y", 1), shift(packed, "y", -1)
    above, below, packed, up, down = lax.optimization_barrier((above, below, packed, up, down))
    low, high = shift(up[:half], "x", 1), shift(down[half:], "x", -1)
    early = [p for a in (tokens, up, down) for p in (a, shift(a, "c", 1))]
    sums = project_early(feature(0, 1, 3, 2), early, key_weight, value_weight)
    low, high, *sums = lax.optimization_barrier((low, high, *sums))
    late = [low, high, shift(low, "c", 1), shift(high, "c", 1)]
    rows = project_late(late, sums, key_weight.shape[0])
    table = [
        ((pair * NZ + k) * BLOCK + r, a)
        for pair in range(PAIRS)
        for k, r, a in ring_pieces(rows[pair], "z")
    ]

    after, _ = lax.optimization_barrier((packed, table[3][1]))
    asked = [packed, above, shift(after, "y", 2), below]

    held_back, _ = lax.optimization_barrier((out_weight, rows[0]))
    weight = lax.all_gather(held_back, ("x", "c"), axis=0, tiled=True)

    wanted = jnp.stack([a[QROWS, : 2 * SPANS_DEV] for a in asked]).astype(jnp.int32)
    shard, row = wanted // ENTRIES, wanted % ENTRIES
    bias = jnp.where(shard // NZ == y, 0.0, FAR).astype(jnp.float32)
    place = (((row // 2) * NZ + (z + NZ - shard % NZ) % NZ) * BLOCK).astype(jnp.int32)
    lane = ((row % 2) * NLEN).astype(jnp.int32)
    messages = [None] * NY
    for k in (2, 1, 3, 0):
        out = attend(place[k], lane[k], bias[k], asked[k], table)
        messages[k] = shift(out, "y", -k) if k else out
    heads_out = combine(lambda_head, messages)

    heads = lax.all_to_all(
        heads_out.reshape(NX * NC, SPAN, WIDE), ("x", "c"), split_axis=0, concat_axis=0, tiled=True
    )
    return output(heads, weight)


def solution(mesh):
    fine = Mesh(mesh.devices.reshape(NY, NZ, NX, NC), ("y", "z", "x", "c"))
    db, tp = ("y", "z"), ("x", "c")
    return jax.shard_map(
        on_device,
        mesh=fine,
        in_specs=(
            P(db, tp),
            P(db, None),
            P(db, None),
            P(db, None, tp),
            P(None, tp),
            P(None, tp),
            P(tp),
            P(tp, None),
        ),
        out_specs=P(db + tp, None),
        check_vma=False,
    )
```
